32 devices in a mesh: front: 4 (over y, core), row: 4 (over z), col: 2 (over x).
Axes of the slice: x: 2, y: 2, z: 4, core: 2. Of those that a mesh axis runs over, the one named last changes fastest.
Arguments:
- front_matrix: float32 [4, 8192, 8192], P('front', 'row', 'col'), may hold values from -16 to 9216
- child_blocks: bfloat16 [4, 2, 6144, 6144], P('front', None, 'row', 'col'), may hold values from -6 to 6
- child_maps: int32 [4, 2, 48], replicated, may hold values from 0 to 63, as said below
- pivot_rows: int32 [4, 16], replicated, may hold values from 0 to 15, as said below
Outputs:
- factored: float32 [4, 8192, 8192], P('front', 'row', 'col')
The draws below stay inside these ranges and needn't reach their ends.
Inputs may be any that keep to these rules, and one draw needn't show every extreme that they name: Each row of pivot_rows is a permutation of 0 to 15. Within each child the entries increase, and entry b lies in the same one of 4 equal segments as b: child_maps[f, s, b] div (16) = b div (12).
All inputs are finite; a program needn't handle non-finite values.
Results may differ from the reference program's by a relative error of at most 0.0027.
Values may be sent and summed in bfloat16 or wider, within the bound.
No kernel may reach another device: no remote copies, remote signals or barrier semaphores. Data moves between devices by JAX's collectives and lax.ppermute only.
A program may use at most 256 MiB of HBM per device.

```python
import jax
import jax.numpy as jnp
import numpy as np
from jax import lax

NF = 8192
W = 512
NP = 2
NCB = 6144
MB = 128
FRONTS = 4
NB = 16
CBLK = 48
SEGS = 4
N_COL = 2


def shuffle_blocks(order_key):
    return jax.random.permutation(order_key, NB).astype(jnp.int32)


def draw_orders(key):
    order_keys = jax.random.split(jax.random.fold_in(key, 7), FRONTS)
    return jax.vmap(shuffle_blocks)(order_keys)


def draw_pivot_rows(key, part):
    return draw_orders(key)


def draw_front(inputs):
    front_key, pivot_cols = inputs
    key_diag, key_block, key_couple = jax.random.split(front_key, 3)
    cell_ids = jnp.arange(NF, dtype=jnp.int32)
    block_ids = cell_ids // W
    within = cell_ids % W
    dominant = pivot_cols[block_ids][:, None] == block_ids[None, :]
    on_diagonal = dominant & (within[:, None] == within[None, :])
    root_width = float(W) ** 0.5
    diag_values = jnp.exp(jax.random.uniform(key_diag, (NF, 1), jnp.float32, jnp.log(9.0 * root_width), jnp.log(18.0 * root_width)))
    block_values = jnp.clip(jax.random.normal(key_block, (NF, NF), jnp.float32), -4.0, 4.0) * 0.4
    coupling = jnp.clip(jax.random.normal(key_couple, (NF, NF), jnp.float32), -4.0, 4.0) * 4.0
    return jnp.where(on_diagonal, diag_values, jnp.where(dominant, block_values, coupling)).astype(jnp.float32)


def draw_front_matrix(key, part):
    order_all = draw_orders(key)
    panel_ids = jnp.arange(NB, dtype=jnp.int32)
    pivot_slabs = panel_ids % N_COL * (NB // N_COL) + panel_ids // N_COL
    position = jnp.zeros((FRONTS, NB), jnp.int32).at[jnp.arange(FRONTS)[:, None], order_all].set(jnp.broadcast_to(panel_ids, (FRONTS, NB)))
    pivot_cols = pivot_slabs[position]
    front_keys = jax.random.split(jax.random.fold_in(key, 11), FRONTS)
    return lax.map(draw_front, (front_keys, pivot_cols))


def draw_child_maps(key, part):
    child_per_seg = CBLK // SEGS
    parent_per_seg = NF // MB // SEGS
    seg_keys = jax.random.split(jax.random.fold_in(key, 13), FRONTS * 2 * SEGS)

    def choose_blocks(seg_key):
        middle = jax.random.permutation(seg_key, parent_per_seg - 2)[:child_per_seg - 2] + 1
        chosen = jnp.concatenate([jnp.zeros((1,), jnp.int32), middle.astype(jnp.int32), jnp.full((1,), parent_per_seg - 1, jnp.int32)])
        return jnp.sort(chosen)
    chosen_all = jax.vmap(choose_blocks)(seg_keys).reshape(FRONTS, 2, SEGS, child_per_seg)
    offsets = (jnp.arange(SEGS, dtype=jnp.int32) * parent_per_seg)[None, None, :, None]
    return (chosen_all + offsets).reshape(FRONTS, 2, CBLK).astype(jnp.int32)


def steps_of(key, shape, shards, least, largest):
    loudness, own = 1.0, jax.random.fold_in(key, 6)
    for axis_at, blocks in shards:
        draws = jnp.exp(jax.random.uniform(jax.random.fold_in(own, axis_at), (blocks,), jnp.float32, least / len(shards), largest / len(shards)))
        loudness = loudness * jnp.repeat(draws, shape[axis_at] // blocks).reshape([-1 if axis == axis_at else 1 for axis in range(len(shape))])
    return loudness


def noise(own_key, shape, deviation, bound, cuts=(), held_as=jnp.bfloat16):
    level = steps_of(own_key, shape, cuts, -0.22, 0.18) if cuts else 1.0
    drawn = jax.random.normal(own_key, shape, jnp.float32) * deviation * level
    return jnp.minimum(jnp.maximum(drawn, -bound), bound).astype(held_as)


def setup_inputs(seed: int = 0) -> dict:
    key_of = jax.random.split(jax.random.key(seed), 5)
    return {
        "front_matrix": draw_front_matrix(jax.random.fold_in(key_of[4], 71), 0),
        "child_blocks": noise(key_of[1], (FRONTS, 2, NCB, NCB), 1.0, 6.0, ((0, 4), (2, 4), (3, 2))),
        "child_maps": draw_child_maps(jax.random.fold_in(key_of[4], 71), 0),
        "pivot_rows": draw_pivot_rows(jax.random.fold_in(key_of[4], 71), 0),
    }


def refine(block):
    reciprocal = 1.0 / jnp.diagonal(block)
    first_guess = 2.0 * jnp.diag(reciprocal) - reciprocal[:, None] * block * reciprocal[None, :]
    product = jnp.dot(block, first_guess, precision=lax.Precision.HIGHEST)
    return 2.0 * first_guess - jnp.dot(first_guess, product, precision=lax.Precision.HIGHEST)


def extend_add(matrix, piece, block_map):
    row_index = (block_map[:, None] * MB + jnp.arange(MB, dtype=jnp.int32)[None, :]).reshape(-1)
    return matrix.at[row_index[:, None], row_index[None, :]].add(piece.astype(jnp.float32))


def slab_of(panel):
    return (panel % N_COL) * (NB // N_COL) + panel // N_COL


def factor_front(matrix, panel_order):
    block_ids = jnp.arange(NB, dtype=jnp.int32)
    for panel in range(NP):
        pivot_index = panel_order[panel]
        slab_start = slab_of(panel) * W
        upper_rows = lax.dynamic_slice_in_dim(matrix, (pivot_index * W).astype(jnp.int32), W, 0)
        inverse = refine(upper_rows[:, slab_start:slab_start + W])
        column = matrix[:, slab_start:slab_start + W]
        done_rows = jnp.repeat(jnp.any(block_ids[:, None] == panel_order[None, :panel + 1], axis=1), W)
        earlier = jnp.repeat(jnp.any(block_ids[:, None] == panel_order[None, :panel], axis=1), W)
        current = jnp.repeat(block_ids == pivot_index, W)
        lower_part = jnp.dot(column.astype(jnp.bfloat16), inverse.astype(jnp.bfloat16),
                             preferred_element_type=jnp.float32).astype(jnp.bfloat16)
        lower_part = jnp.where(done_rows[:, None], jnp.zeros((), jnp.bfloat16), lower_part)
        done_slabs = np.zeros(NB, dtype=bool)
        for earlier_panel in range(panel + 1):
            done_slabs[slab_of(earlier_panel)] = True
        done_cols = jnp.asarray(np.repeat(done_slabs, W))
        upper_part = jnp.where(done_cols[None, :], jnp.zeros((), jnp.bfloat16), upper_rows.astype(jnp.bfloat16))
        matrix = matrix - jnp.dot(lower_part, upper_part, preferred_element_type=jnp.float32)
        new_slab = jnp.where(earlier[:, None], column,
                             jnp.where(current[:, None], jnp.tile(inverse, (NB, 1)), lower_part.astype(jnp.float32)))
        matrix = matrix.at[:, slab_start:slab_start + W].set(new_slab)
    return matrix


def reference(front_matrix, child_blocks, child_maps, pivot_rows):
    results = []
    for front_index in range(FRONTS):
        matrix = front_matrix[front_index]
        matrix = extend_add(matrix, child_blocks[front_index, 0], child_maps[front_index, 0])
        matrix = extend_add(matrix, child_blocks[front_index ^ 1, 1], child_maps[front_index ^ 1, 1])
        results.append(factor_front(matrix, pivot_rows[front_index]))
    return jnp.stack(results)
```

```python
import functools

import jax
import jax.numpy as jnp
from jax import lax
from jax.experimental import pallas as pl
from jax.experimental.pallas import tpu as pltpu
from jax.sharding import PartitionSpec as P

W = 512
MB = 128
CH = 256
PB = W // MB
TILE_CHUNKS = W // CH
HBM = pl.BlockSpec(memory_space=pltpu.HBM)
SMEM = pl.BlockSpec(memory_space=pltpu.SMEM)
F32 = jnp.float32
BF16 = jnp.bfloat16
MIB = 1 << 20
VMEM_MIB = 48
VMEM = pl.BlockSpec(memory_space=pltpu.VMEM)

OWNS, DIST, LOCAL, OWN_AT, GOT_AT, SEND_AT, COL, LISTS = 0, 2, 4, 6, 8, 10, 12, 16


class Sizes:
    def __init__(self, rows, cols, front, child):
        self.rows, self.cols = rows, cols
        self.local_rows, self.local_cols = front
        self.child_rows, self.child_cols = child
        self.row_blocks = self.local_rows // W
        self.chunks = self.local_cols // CH
        self.map_rows, self.map_cols = self.local_rows // MB, self.local_cols // MB
        self.own_row = LISTS
        self.got_row = self.own_row + self.map_rows
        self.own_col = self.got_row + self.map_rows
        self.got_col = self.own_col + self.map_cols
        self.plan = self.got_col + self.map_cols


def params(mib):
    return pltpu.CompilerParams(vmem_limit_bytes=mib * MIB)


def make_plan(sz, ids, child_maps, pivot_rows):
    child_row_blocks = sz.child_rows // MB
    child_col_blocks = sz.child_cols // MB

    def place(z):
        return jnp.where(z % 2 == 1, (z + 1) // 2, jnp.where(z == 0, 0, sz.rows - z // 2))

    def kernel(ids_ref, maps_ref, order_ref, out_ref):
        front, row, col = ids_ref[0], ids_ref[1], ids_ref[2]
        partner = jnp.bitwise_xor(front, 1)
        for i in range(COL + 1, LISTS):
            out_ref[i] = 0
        out_ref[COL] = col

        def start(f, s, local):
            count = jnp.int32(0)
            for b in range(child_row_blocks):
                at = maps_ref[f, s, row * child_row_blocks + b] - row * sz.map_rows
                count += (at < local * PB).astype(jnp.int32)
            return jnp.minimum(count, child_row_blocks - PB)

        for p in range(2):
            pivot = order_ref[front, p]
            owner = pivot // sz.row_blocks
            local = pivot - owner * sz.row_blocks
            other = order_ref[partner, p] % sz.row_blocks
            out_ref[OWNS + p] = (owner == row).astype(jnp.int32)
            out_ref[DIST + p] = (place(row) - place(owner) + sz.rows) % sz.rows
            out_ref[LOCAL + p] = local
            out_ref[OWN_AT + p] = start(front, 0, local)
            out_ref[GOT_AT + p] = start(partner, 1, local)
            out_ref[SEND_AT + p] = start(front, 1, other)
        for f, s, row_list, col_list in (
            (front, 0, sz.own_row, sz.own_col),
            (partner, 1, sz.got_row, sz.got_col),
        ):
            for i in range(sz.map_rows):
                out_ref[row_list + i] = -1
            for i in range(sz.map_cols):
                out_ref[col_list + i] = -1
            for b in range(child_row_blocks):
                at = maps_ref[f, s, row * child_row_blocks + b] - row * sz.map_rows
                out_ref[row_list + at] = b
            for b in range(child_col_blocks):
                at = maps_ref[f, s, col * child_col_blocks + b] - col * sz.map_cols
                out_ref[col_list + at] = b

    return pl.pallas_call(
        kernel,
        out_shape=jax.ShapeDtypeStruct((sz.plan,), jnp.int32),
        in_specs=[SMEM] * 3,
        out_specs=SMEM,
        compiler_params=params(VMEM_MIB),
        name="plan",
    )(ids, child_maps, pivot_rows)


def cut_rows(sz, plan, child_blocks, panel):
    def kernel(plan_ref, child_ref, out_ref, sem):
        at = pl.multiple_of(plan_ref[SEND_AT + panel] * MB, MB)
        copy = pltpu.make_async_copy(child_ref.at[0, 1, pl.ds(at, W)], out_ref, sem)
        copy.start()
        copy.wait()

    return pl.pallas_call(
        kernel,
        out_shape=jax.ShapeDtypeStruct((W, sz.child_cols), BF16),
        in_specs=[SMEM, HBM],
        out_specs=VMEM,
        scratch_shapes=[pltpu.SemaphoreType.DMA],
        compiler_params=params(VMEM_MIB),
        name="cut_rows",
    )(plan, child_blocks)


def cut_cols(sz, child_blocks):
    def kernel(child_ref, out_ref, sem):
        copy = pltpu.make_async_copy(child_ref.at[0, 1, :, pl.ds(0, W)], out_ref, sem)
        copy.start()
        copy.wait()

    return pl.pallas_call(
        kernel,
        out_shape=jax.ShapeDtypeStruct((sz.child_rows, W), BF16),
        in_specs=[HBM],
        out_specs=VMEM,
        scratch_shapes=[pltpu.SemaphoreType.DMA],
        compiler_params=params(VMEM_MIB),
        name="cut_cols",
    )(child_blocks)


def place_of(row, col):
    there = jnp.logical_and(row >= 0, col >= 0).astype(F32)
    row_at = pl.multiple_of(jnp.maximum(row, 0) * MB, MB)
    col_at = pl.multiple_of(jnp.maximum(col, 0) * MB, MB)
    return pl.ds(row_at, MB), pl.ds(col_at, MB), there


def pivot_panel(sz, plan, front_matrix, child_blocks, got_rows, panel):
    group = max(g for g in (1, 2, 4) if sz.chunks % g == 0)
    wide = group * CH

    def kernel(plan_ref, front_ref, child_ref, got_ref, rows_ref, tile_ref, own_ref, sem):
        j = pl.program_id(0)
        own_at, got_at = plan_ref[OWN_AT + panel], plan_ref[GOT_AT + panel]
        local = plan_ref[LOCAL + panel]

        @pl.when(j == 0)
        def _():
            at = pl.multiple_of(own_at * MB, MB)
            copy = pltpu.make_async_copy(child_ref.at[0, 0, pl.ds(at, W)], own_ref, sem)
            copy.start()
            copy.wait()

        def value_of(i, q):
            own_col = plan_ref[sz.own_col + j * (wide // MB) + q]
            got_col = plan_ref[sz.got_col + j * (wide // MB) + q]
            r1, c1, f1 = place_of(plan_ref[sz.own_row + local * PB + i] - own_at, own_col)
            r2, c2, f2 = place_of(plan_ref[sz.got_row + local * PB + i] - got_at, got_col)
            value = front_ref[0, pl.ds(i * MB, MB), pl.ds(q * MB, MB)]
            value += own_ref[r1, c1].astype(F32) * f1
            return value + got_ref[r2, c2].astype(F32) * f2

        for q in range(wide // MB):
            for i in range(PB):
                here = pl.ds(q * MB % CH, MB)
                rows_ref[q * MB // CH, pl.ds(i * MB, MB), here] = value_of(i, q).astype(BF16)

        @pl.when(j < max(W // wide, 1))
        def _():
            for q in range(min(wide, W) // MB):
                for i in range(PB):
                    tile_ref[pl.ds(i * MB, MB), pl.ds(q * MB, MB)] = value_of(i, q)

    last_tile = max(W // wide, 1) - 1
    return pl.pallas_call(
        kernel,
        out_shape=(
            jax.ShapeDtypeStruct((sz.chunks, W, CH), BF16),
            jax.ShapeDtypeStruct((W, W), F32),
        ),
        grid_spec=pltpu.PrefetchScalarGridSpec(
            num_scalar_prefetch=1,
            grid=(sz.chunks // group,),
            in_specs=[
                pl.BlockSpec((1, W, wide), lambda j, plan: (0, plan[LOCAL + panel], j)),
                HBM,
                pl.BlockSpec((W, sz.child_cols), lambda j, plan: (0, 0)),
            ],
            out_specs=[
                pl.BlockSpec((group, W, CH), lambda j, plan: (j, 0, 0)),
                pl.BlockSpec((W, min(wide, W)), lambda j, plan: (0, jnp.minimum(j, last_tile))),
            ],
            scratch_shapes=[pltpu.VMEM((W, sz.child_cols), BF16), pltpu.SemaphoreType.DMA],
        ),
        compiler_params=params(VMEM_MIB),
        cost_estimate=pl.CostEstimate(flops=0, bytes_accessed=20 * MIB, transcendentals=0),
        name="pivot_panel",
    )(plan, front_matrix, child_blocks, got_rows)


def first_columns(sz, plan, front_matrix, child_blocks, got_cols):
    def kernel(plan_ref, front_ref, own_ref, got_ref, out_ref):
        r = pl.program_id(0)
        for i in range(PB):
            own_row = plan_ref[sz.own_row + r * PB + i]
            got_row = plan_ref[sz.got_row + r * PB + i]
            for q in range(PB):
                r1, c1, f1 = place_of(own_row, plan_ref[sz.own_col + q])
                r2, c2, f2 = place_of(got_row, plan_ref[sz.got_col + q])
                here = (pl.ds(i * MB, MB), pl.ds(q * MB, MB))
                value = front_ref[0, here[0], here[1]] + own_ref[r1, c1].astype(F32) * f1
                value += got_ref[r2, c2].astype(F32) * f2
                out_ref[here] = value.astype(BF16)

    return pl.pallas_call(
        kernel,
        out_shape=jax.ShapeDtypeStruct((sz.local_rows, W), BF16),
        grid_spec=pltpu.PrefetchScalarGridSpec(
            num_scalar_prefetch=1,
            grid=(sz.row_blocks,),
            in_specs=[
                pl.BlockSpec((1, W, W), lambda r, plan: (0, r, 0)),
                pl.BlockSpec((None, None, sz.child_rows, W), lambda r, plan: (0, 0, 0, 0)),
                pl.BlockSpec((sz.child_rows, W), lambda r, plan: (0, 0)),
            ],
            out_specs=pl.BlockSpec((W, W), lambda r, plan: (r, 0)),
        ),
        compiler_params=params(VMEM_MIB),
        cost_estimate=pl.CostEstimate(flops=0, bytes_accessed=10 * MIB, transcendentals=0),
        name="first_columns",
    )(plan, front_matrix, child_blocks, got_cols)


def begin(panel_rows):
    def kernel(rows_ref, out_ref, sem):
        copy = pltpu.make_async_copy(rows_ref.at[0], out_ref, sem)
        copy.start()
        copy.wait()

    return pl.pallas_call(
        kernel,
        out_shape=jax.ShapeDtypeStruct(panel_rows.shape[1:], BF16),
        in_specs=[HBM],
        out_specs=VMEM,
        scratch_shapes=[pltpu.SemaphoreType.DMA],
        compiler_params=params(VMEM_MIB),
        name="begin",
    )(panel_rows)


def inject(plan, panel_rows, panel, chunk, received):
    put_in = chunk < panel_rows.shape[0]

    def kernel(plan_ref, rows_ref, received_ref, out_ref, held_ref, sems):
        if put_in:

            @pl.when(plan_ref[OWNS + panel] == 1)
            def _():
                for n, (source, target) in enumerate(
                    ((rows_ref.at[chunk], held_ref), (held_ref, out_ref))
                ):
                    copy = pltpu.make_async_copy(source, target, sems.at[n])
                    copy.start()
                    copy.wait()

    return pl.pallas_call(
        kernel,
        out_shape=jax.ShapeDtypeStruct(received.shape, BF16),
        in_specs=[SMEM, HBM, HBM],
        out_specs=HBM,
        scratch_shapes=[pltpu.VMEM(received.shape, BF16), pltpu.SemaphoreType.DMA((2,))],
        input_output_aliases={2: 0},
        compiler_params=params(VMEM_MIB),
        name="inject",
    )(plan, panel_rows, received)


def gather_tiles(sz, plan, passed):
    count = len(passed[0])

    def kernel(plan_ref, *refs):
        sources = (refs[:count], refs[count : 2 * count])
        out_ref, sems = refs[2 * count :]
        for p in range(2):
            for d in range(sz.rows):

                @pl.when(plan_ref[DIST + p] == d)
                def _():
                    for t in range(TILE_CHUNKS):
                        pltpu.make_async_copy(
                            sources[p][t + d], out_ref.at[p, t], sems.at[p, t]
                        ).start()

        for p in range(2):
            for t in range(TILE_CHUNKS):
                pltpu.make_async_copy(sources[p][t], out_ref.at[p, t], sems.at[p, t]).wait()

    return pl.pallas_call(
        kernel,
        out_shape=jax.ShapeDtypeStruct((2, TILE_CHUNKS, W, CH), BF16),
        in_specs=[SMEM] + [HBM] * (2 * count),
        out_specs=VMEM,
        scratch_shapes=[pltpu.SemaphoreType.DMA((2, TILE_CHUNKS))],
        compiler_params=params(VMEM_MIB),
        name="gather_tiles",
    )(plan, *passed[0], *passed[1])


def invert(block):
    rows = lax.broadcasted_iota(jnp.int32, (W, W), 0)
    cols = lax.broadcasted_iota(jnp.int32, (W, W), 1)
    on_diagonal = rows == cols
    diagonal = jnp.where(on_diagonal, block, 0.0)
    down = 1.0 / jnp.sum(diagonal, axis=1, keepdims=True)
    across = 1.0 / jnp.sum(diagonal, axis=0, keepdims=True)
    first = jnp.where(on_diagonal, 2.0 * down, 0.0) - down * block * across
    product = jnp.dot(block, first, precision=lax.Precision.HIGHEST, preferred_element_type=F32)
    return 2.0 * first - jnp.dot(
        first, product, precision=lax.Precision.HIGHEST, preferred_element_type=F32
    )


def tile_algebra(sz, plan, tiles_0, tiles_1, exact_0, exact_1):
    def tile(ref, p):
        return jnp.concatenate([ref[p, t] for t in range(TILE_CHUNKS)], axis=1)

    def kernel(plan_ref, t0_ref, t1_ref, e0_ref, e1_ref, x0_ref, x1_ref, h0_ref, h1_ref, l_ref):
        col = plan_ref[COL]
        mine_0 = jnp.logical_and(plan_ref[OWNS] == 1, col == 0)
        mine_1 = jnp.logical_and(plan_ref[OWNS + 1] == 1, col == 1)
        x0 = invert(jnp.where(mine_0, e0_ref[...], tile(t0_ref, 0).astype(F32)))
        x0_ref[...] = x0
        h0_ref[...] = x0.astype(BF16)
        lower = jnp.dot(tile(t0_ref, 1), h0_ref[...], preferred_element_type=F32).astype(BF16)
        l_ref[...] = lower
        block = jnp.where(mine_1, e1_ref[...], tile(t1_ref, 1).astype(F32))
        block -= jnp.dot(lower, tile(t1_ref, 0), preferred_element_type=F32)
        x1 = invert(block)
        x1_ref[...] = x1
        h1_ref[...] = x1.astype(BF16)

    return pl.pallas_call(
        kernel,
        out_shape=[jax.ShapeDtypeStruct((W, W), t) for t in (F32, F32, BF16, BF16, BF16)],
        in_specs=[SMEM] + [VMEM] * 4,
        out_specs=[VMEM] * 5,
        compiler_params=params(VMEM_MIB),
        name="tile_algebra",
    )(plan, tiles_0, tiles_1, exact_0, exact_1)


def is_pivot(plan_ref, panel, r):
    return jnp.logical_and(plan_ref[OWNS + panel] == 1, plan_ref[LOCAL + panel] == r)


def multipliers(sz, plan, cols_0, cols_1, half_0, half_1, tiles_1):
    def kernel(plan_ref, c0_ref, c1_ref, h0_ref, h1_ref, t1_ref, out_ref):
        r = pl.program_id(0)
        keep_0 = 1.0 - is_pivot(plan_ref, 0, r).astype(F32)
        keep_1 = keep_0 * (1.0 - is_pivot(plan_ref, 1, r).astype(F32))
        upper = jnp.concatenate([t1_ref[0, t] for t in range(TILE_CHUNKS)], axis=1)
        lower_0 = jnp.dot(c0_ref[...], h0_ref[...], preferred_element_type=F32) * keep_0
        lower_0 = lower_0.astype(BF16)
        column = c1_ref[...].astype(F32) - jnp.dot(lower_0, upper, preferred_element_type=F32)
        lower_1 = jnp.dot(column.astype(BF16), h1_ref[...], preferred_element_type=F32) * keep_1
        out_ref[:, :W] = lower_0
        out_ref[:, W:] = lower_1.astype(BF16)

    whole = pl.BlockSpec((W, W), lambda r, plan: (0, 0))
    part = pl.BlockSpec((W, W), lambda r, plan: (r, 0))
    return pl.pallas_call(
        kernel,
        out_shape=jax.ShapeDtypeStruct((sz.local_rows, 2 * W), BF16),
        grid_spec=pltpu.PrefetchScalarGridSpec(
            num_scalar_prefetch=1,
            grid=(sz.row_blocks,),
            in_specs=[
                part,
                part,
                whole,
                whole,
                pl.BlockSpec((2, TILE_CHUNKS, W, CH), lambda r, plan: (0, 0, 0, 0)),
            ],
            out_specs=pl.BlockSpec((W, 2 * W), lambda r, plan: (r, 0)),
        ),
        compiler_params=params(VMEM_MIB),
        cost_estimate=pl.CostEstimate(
            flops=6 * sz.local_rows * W * W, bytes_accessed=10 * MIB, transcendentals=0
        ),
        name="multipliers",
    )(plan, cols_0, cols_1, half_0, half_1, tiles_1)


def update(sz, plan, chunk, front_matrix, child_blocks, partner, lower, lower_1, passed, exact, out):
    special = chunk < TILE_CHUNKS
    per = CH // MB
    blocks = sz.row_blocks
    columns = pl.ds(chunk * CH, CH)

    def kernel(plan_ref, front_ref, own_ref, partner_ref, lower_ref, low_ref, *refs):
        sources = (refs[: sz.rows], refs[sz.rows : 2 * sz.rows])
        refs = refs[2 * sz.rows :]
        if special:
            exact_refs, refs = refs[:2], refs[2:]
        out_ref, f_buf, l_buf, c_buf, x_buf, upper, raw, low, o_buf, sems = refs[-10:]
        targets = (upper.at[pl.ds(0, W)], raw)

        for p in range(2):
            for d in range(sz.rows):

                @pl.when(plan_ref[DIST + p] == d)
                def _():
                    pltpu.make_async_copy(sources[p][d], targets[p], sems.at[p]).start()

        head = [pltpu.make_async_copy(sources[p][0], targets[p], sems.at[p]) for p in range(2)]
        head.append(pltpu.make_async_copy(low_ref, low, sems.at[2]))
        head[2].start()
        children = []
        for n, (child, which, at) in enumerate(
            ((own_ref, 0, sz.own_col), (partner_ref, 1, sz.got_col))
        ):
            for q in range(per):
                b = jnp.maximum(plan_ref[at + chunk * per + q], 0)
                b = pl.ds(pl.multiple_of(b * MB, MB), MB)
                children.append(
                    pltpu.make_async_copy(
                        child.at[0, which, :, b], c_buf.at[n, q], sems.at[3 + n * per + q]
                    )
                )
                children[-1].start()
        base = 3 + 2 * per
        if special:
            for p in range(2):
                children.append(
                    pltpu.make_async_copy(
                        exact_refs[p].at[:, columns], x_buf.at[p], sems.at[base + p]
                    )
                )
                children[-1].start()
        base += 2
        loads, stores = [], []
        for r in range(blocks):
            rows = pl.ds(r * W, W)
            loads.append(
                (
                    pltpu.make_async_copy(
                        front_ref.at[0, rows, columns], f_buf.at[rows], sems.at[base + 3 * r]
                    ),
                    pltpu.make_async_copy(
                        lower_ref.at[rows], l_buf.at[rows], sems.at[base + 3 * r + 1]
                    ),
                )
            )
            stores.append(
                pltpu.make_async_copy(
                    o_buf.at[rows], out_ref.at[0, rows, columns], sems.at[base + 3 * r + 2]
                )
            )
            for copy in loads[-1]:
                copy.start()
        for copy in head:
            copy.wait()
        product = jnp.dot(low[...], upper[:W], preferred_element_type=F32)
        upper[W:] = (raw[...].astype(F32) - product).astype(BF16)
        for copy in children:
            copy.wait()
        for r in range(blocks):
            for copy in loads[r]:
                copy.wait()
            product = jnp.dot(l_buf[r * W : (r + 1) * W], upper[...], preferred_element_type=F32)
            for q in range(per):
                here = pl.ds(q * MB, MB)
                own_col = plan_ref[sz.own_col + chunk * per + q]
                got_col = plan_ref[sz.got_col + chunk * per + q]
                for i in range(PB):
                    rows = pl.ds(r * W + i * MB, MB)
                    r1, _, f1 = place_of(plan_ref[sz.own_row + r * PB + i], own_col)
                    r2, _, f2 = place_of(plan_ref[sz.got_row + r * PB + i], got_col)
                    value = f_buf[rows, here] + c_buf[0, q, r1, :].astype(F32) * f1
                    value += c_buf[1, q, r2, :].astype(F32) * f2
                    value -= product[i * MB : (i + 1) * MB, q * MB : (q + 1) * MB]
                    o_buf[rows, here] = value
            if special:
                col = plan_ref[COL]
                first, second = is_pivot(plan_ref, 0, r), is_pivot(plan_ref, 1, r)
                rows = pl.ds(r * W, W)

                @pl.when(jnp.logical_and(col == 0, first))
                def _():
                    o_buf[rows] = x_buf[0]

                @pl.when(jnp.logical_and(col == 0, jnp.logical_not(first)))
                def _():
                    o_buf[rows] = l_buf[rows, columns].astype(F32)

                @pl.when(jnp.logical_and(col == 1, second))
                def _():
                    o_buf[rows] = x_buf[1]

                @pl.when(jnp.logical_and(col == 1, jnp.logical_not(jnp.logical_or(first, second))))
                def _():
                    o_buf[rows] = l_buf[rows, pl.ds(W + chunk * CH, CH)].astype(F32)

            stores[r].start()
        for copy in stores:
            copy.wait()

    operands = [plan, front_matrix, child_blocks, partner, lower, lower_1]
    operands += list(passed[0]) + list(passed[1])
    if special:
        operands += list(exact)
    aliases = {}
    if out is not None:
        aliases = {len(operands): 0}
        operands.append(out)
    return pl.pallas_call(
        kernel,
        out_shape=jax.ShapeDtypeStruct(front_matrix.shape, F32),
        in_specs=[SMEM] + [HBM] * (len(operands) - 1),
        out_specs=HBM,
        scratch_shapes=[
            pltpu.VMEM((sz.local_rows, CH), F32),
            pltpu.VMEM((sz.local_rows, 2 * W), BF16),
            pltpu.VMEM((2, per, sz.child_rows, MB), BF16),
            pltpu.VMEM((2, W, CH), F32),
            pltpu.VMEM((2 * W, CH), BF16),
            pltpu.VMEM((W, CH), BF16),
            pltpu.VMEM((W, W), BF16),
            pltpu.VMEM((sz.local_rows, CH), F32),
            pltpu.SemaphoreType.DMA((5 + 2 * per + 3 * blocks,)),
        ],
        input_output_aliases=aliases,
        compiler_params=params(VMEM_MIB),
        cost_estimate=pl.CostEstimate(
            flops=4 * sz.local_rows * W * CH, bytes_accessed=10 * MIB, transcendentals=0
        ),
        name="update",
    )(*operands)


def tie(value, *after):
    return lax.optimization_barrier((value, *after))[0]


def from_first_two(cols, col, mine):
    if cols == 2:
        other = lax.ppermute(mine, "col", [(0, 1), (1, 0)])
        return jnp.where(col == 0, mine, other), jnp.where(col == 0, other, mine)
    zero = jnp.zeros_like(mine)
    return tuple(lax.psum(jnp.where(col == c, mine, zero), "col") for c in range(2))


def body(rows, cols, front_matrix, child_blocks, child_maps, pivot_rows):
    sz = Sizes(rows, cols, front_matrix.shape[1:], child_blocks.shape[2:])
    front_count = lax.axis_size("front")
    swap = [(f, f ^ 1) for f in range(front_count)]
    order = [0] + list(range(1, rows, 2)) + sorted(range(2, rows, 2), reverse=True)
    ring = [(order[i], order[(i + 1) % rows]) for i in range(rows)]
    col = lax.axis_index("col")
    ids = jnp.stack([lax.axis_index("front"), lax.axis_index("row"), col]).astype(jnp.int32)
    plan = make_plan(sz, ids, child_maps, pivot_rows)

    got_0 = lax.ppermute(cut_rows(sz, plan, child_blocks, 0), "front", swap)
    rows_0, exact_0 = pivot_panel(sz, plan, front_matrix, child_blocks, got_0, 0)
    got_1 = lax.ppermute(cut_rows(sz, plan, tie(child_blocks, got_0), 1), "front", swap)
    rows_1, exact_1 = pivot_panel(sz, plan, front_matrix, child_blocks, got_1, 1)
    panel_rows = (rows_0, rows_1)

    steps = sz.chunks + rows - 2
    turns = 2 * steps
    tiles_turn = min(2 * rows + 1, turns - 1)
    algebra_turn = min(tiles_turn + 7, turns - 1)
    passed = ([], [])
    held = [None, None]
    state = {"chunk": 0, "out": None}
    after = ()
    partner = None

    def next_update():
        t = state["chunk"]
        state["chunk"] = t + 1
        at = [passed[p][t : t + rows] for p in range(2)]
        state["out"] = update(
            sz, plan, t, front_matrix, child_blocks, partner, lower, lower_1, at, exact, state["out"]
        )

    for turn in range(turns):
        s, k = turn // 2, turn % 2
        if s == 0:
            held[k] = begin(tie(panel_rows[k], *after))
        else:
            held[k] = inject(plan, panel_rows[k], k, s, tie(held[k], *after))
        after = ()
        passed[k].append(held[k])
        if turn == 0:
            send = cut_cols(sz, tie(child_blocks, got_1, held[0]))
            got_cols = lax.ppermute(send, "front", swap)
        held[k] = lax.ppermute(held[k], "row", ring)
        if turn == 1:
            mine = first_columns(sz, plan, front_matrix, child_blocks, tie(got_cols, passed[1][0]))
            partner = lax.ppermute(tie(child_blocks, mine), "front", swap)
            cols_0, cols_1 = from_first_two(cols, col, mine)
            after = (mine,)
        if turn == tiles_turn:
            tiles = gather_tiles(sz, plan, [passed[p][: TILE_CHUNKS + rows - 1] for p in range(2)])
            tiles_0, tiles_1 = from_first_two(cols, col, tiles)
            after = (tiles,)
        if turn == algebra_turn:
            *exact, half_0, half_1, lower_1 = tile_algebra(
                sz, plan, tiles_0, tiles_1, exact_0, exact_1
            )
            after = (lower_1,)
        if turn == algebra_turn + 1 or turn == algebra_turn == turns - 1:
            lower = multipliers(sz, plan, cols_0, cols_1, half_0, half_1, tiles_1)
            after = (lower,)
        if turn > algebra_turn + 1 and 2 * (state["chunk"] + rows - 1) + 1 <= turn:
            next_update()
            after = (state["out"],)
    for k in range(2):
        passed[k].append(held[k])
    while state["chunk"] < sz.chunks:
        next_update()
    return state["out"]


def solution(mesh):
    in_specs = (P("front", "row", "col"), P("front", None, "row", "col"), P(), P())
    out_specs = P("front", "row", "col")
    step = functools.partial(body, mesh.shape["row"], mesh.shape["col"])
    return jax.shard_map(step, mesh=mesh, in_specs=in_specs, out_specs=out_specs, check_vma=False)
```

```python
import functools

import jax
import jax.numpy as jnp
from jax import lax
from jax.experimental import pallas as pl
from jax.experimental.pallas import tpu as pltpu
from jax.sharding import PartitionSpec as P

W = 512
MB = 128
CH = 256
PB = W // MB
TILE_CHUNKS = W // CH
EARLY_CHUNKS = 4
PARTS = 2
HBM = pl.BlockSpec(memory_space=pltpu.HBM)
SMEM = pl.BlockSpec(memory_space=pltpu.SMEM)
TILE_SPEC = pl.BlockSpec((W, W), lambda i: (0, 0))
TILES_SPEC = pl.BlockSpec((2, TILE_CHUNKS, W, CH), lambda i: (0, 0, 0, 0))
F32 = jnp.float32
BF16 = jnp.bfloat16
MIB = 1 << 20
VMEM_MIB = 48
FULL_MIB = 60
VMEM = pl.BlockSpec(memory_space=pltpu.VMEM)

OWNS, DIST, LOCAL, OWN_AT, GOT_AT, SEND_AT, COL, FLIP, LISTS = 0, 2, 4, 6, 8, 10, 12, 13, 16


class Sizes:
    def __init__(self, rows, cols, front, child):
        self.rows, self.cols = rows, cols
        self.local_rows, self.local_cols = front
        self.child_rows, self.child_cols = child
        self.row_blocks = self.local_rows // W
        self.chunks = self.local_cols // CH
        self.map_rows, self.map_cols = self.local_rows // MB, self.local_cols // MB
        self.own_row = LISTS
        self.got_row = self.own_row + self.map_rows
        self.own_col = self.got_row + self.map_rows
        self.got_col = self.own_col + self.map_cols
        self.plan = self.got_col + self.map_cols


def params(mib):
    return pltpu.CompilerParams(vmem_limit_bytes=mib * MIB)


def make_plan(sz, ids, child_maps, pivot_rows):
    child_row_blocks = sz.child_rows // MB
    child_col_blocks = sz.child_cols // MB

    def place(z):
        return jnp.where(z % 2 == 1, (z + 1) // 2, jnp.where(z == 0, 0, sz.rows - z // 2))

    def kernel(ids_ref, maps_ref, order_ref, out_ref):
        front, row, col = ids_ref[0], ids_ref[1], ids_ref[2]
        partner = jnp.bitwise_xor(front, 1)
        for i in range(FLIP + 1, LISTS):
            out_ref[i] = 0
        out_ref[COL] = col
        out_ref[FLIP] = col if sz.cols == 2 else jnp.int32(0)

        def start(f, s, local):
            count = jnp.int32(0)
            for b in range(child_row_blocks):
                at = maps_ref[f, s, row * child_row_blocks + b] - row * sz.map_rows
                count += (at < local * PB).astype(jnp.int32)
            return jnp.minimum(count, child_row_blocks - PB)

        for p in range(2):
            pivot = order_ref[front, p]
            owner = pivot // sz.row_blocks
            local = pivot - owner * sz.row_blocks
            other = order_ref[partner, p] % sz.row_blocks
            out_ref[OWNS + p] = (owner == row).astype(jnp.int32)
            out_ref[DIST + p] = (place(row) - place(owner) + sz.rows) % sz.rows
            out_ref[LOCAL + p] = local
            out_ref[OWN_AT + p] = start(front, 0, local)
            out_ref[GOT_AT + p] = start(partner, 1, local)
            out_ref[SEND_AT + p] = start(front, 1, other)
        for f, s, row_list, col_list in (
            (front, 0, sz.own_row, sz.own_col),
            (partner, 1, sz.got_row, sz.got_col),
        ):
            for i in range(sz.map_rows):
                out_ref[row_list + i] = -1
            for i in range(sz.map_cols):
                out_ref[col_list + i] = -1
            for b in range(child_row_blocks):
                at = maps_ref[f, s, row * child_row_blocks + b] - row * sz.map_rows
                out_ref[row_list + at] = b
            for b in range(child_col_blocks):
                at = maps_ref[f, s, col * child_col_blocks + b] - col * sz.map_cols
                out_ref[col_list + at] = b

    return pl.pallas_call(
        kernel,
        out_shape=jax.ShapeDtypeStruct((sz.plan,), jnp.int32),
        in_specs=[SMEM] * 3,
        out_specs=SMEM,
        compiler_params=params(FULL_MIB),
        name="plan",
    )(ids, child_maps, pivot_rows)


def cut_rows(sz, plan, child_blocks, columns):
    def kernel(plan_ref, child_ref, out_ref, sems):
        copies = []
        for p in range(2):
            at = pl.multiple_of(plan_ref[SEND_AT + p] * MB, MB)
            source = child_ref.at[0, 1, pl.ds(at, W), pl.ds(0, columns)]
            copies.append(pltpu.make_async_copy(source, out_ref.at[p], sems.at[p]))
            copies[-1].start()
        for copy in copies:
            copy.wait()

    return pl.pallas_call(
        kernel,
        out_shape=jax.ShapeDtypeStruct((2, W, columns), BF16),
        in_specs=[SMEM, HBM],
        out_specs=VMEM,
        scratch_shapes=[pltpu.SemaphoreType.DMA((2,))],
        compiler_params=params(VMEM_MIB),
        cost_estimate=pl.CostEstimate(flops=0, bytes_accessed=10 * MIB, transcendentals=0),
        name="cut_rows",
    )(plan, child_blocks)


def cut_cols(sz, child_blocks):
    def kernel(child_ref, out_ref, sem):
        copy = pltpu.make_async_copy(child_ref.at[0, 1, :, pl.ds(0, W)], out_ref, sem)
        copy.start()
        copy.wait()

    return pl.pallas_call(
        kernel,
        out_shape=jax.ShapeDtypeStruct((sz.child_rows, W), BF16),
        in_specs=[HBM],
        out_specs=VMEM,
        scratch_shapes=[pltpu.SemaphoreType.DMA],
        compiler_params=params(FULL_MIB),
        name="cut_cols",
    )(child_blocks)


def place_of(row, col):
    there = jnp.logical_and(row >= 0, col >= 0).astype(F32)
    row_at = pl.multiple_of(jnp.maximum(row, 0) * MB, MB)
    col_at = pl.multiple_of(jnp.maximum(col, 0) * MB, MB)
    return pl.ds(row_at, MB), pl.ds(col_at, MB), there


def pivot_chunks(sz, plan, front_matrix, child_blocks, got_rows, panels, first, count):
    columns = got_rows.shape[2]
    tiles = TILE_CHUNKS if first == 0 else 0
    total = len(panels) * count
    exacts = len(panels) if tiles else 0

    def kernel(plan_ref, front_ref, child_ref, got_ref, *refs):
        rows_refs, exact_refs = refs[:total], refs[total : total + exacts]
        own_buf, got_buf, f_buf, o_buf, sems = refs[total + exacts :]
        children, loads, stores = [], [], []
        for n, p in enumerate(panels):
            at = pl.multiple_of(plan_ref[OWN_AT + p] * MB, MB)
            source = child_ref.at[0, 0, pl.ds(at, W), pl.ds(0, columns)]
            children.append(pltpu.make_async_copy(source, own_buf.at[n], sems.at[2 * n]))
            children.append(
                pltpu.make_async_copy(got_ref.at[p], got_buf.at[n], sems.at[2 * n + 1])
            )
        for copy in children:
            copy.start()
        for n, p in enumerate(panels):
            rows = pl.ds(pl.multiple_of(plan_ref[LOCAL + p] * W, W), W)
            for j in range(count):
                at = n * count + j
                base = 4 + 3 * at
                source = front_ref.at[0, rows, pl.ds((first + j) * CH, CH)]
                loads.append(pltpu.make_async_copy(source, f_buf.at[at], sems.at[base]))
                loads[-1].start()
                stores.append(
                    [pltpu.make_async_copy(o_buf.at[at], rows_refs[at], sems.at[base + 1])]
                )
                if j < tiles:
                    target = exact_refs[n].at[:, pl.ds(j * CH, CH)]
                    stores[-1].append(
                        pltpu.make_async_copy(f_buf.at[at], target, sems.at[base + 2])
                    )
        for copy in children:
            copy.wait()
        for n, p in enumerate(panels):
            own_at, got_at = plan_ref[OWN_AT + p], plan_ref[GOT_AT + p]
            local = plan_ref[LOCAL + p]
            for j in range(count):
                at = n * count + j
                loads[at].wait()
                for q in range(CH // MB):
                    here = pl.ds(q * MB, MB)
                    own_col = plan_ref[sz.own_col + (first + j) * (CH // MB) + q]
                    got_col = plan_ref[sz.got_col + (first + j) * (CH // MB) + q]
                    for i in range(PB):
                        own_row = plan_ref[sz.own_row + local * PB + i] - own_at
                        got_row = plan_ref[sz.got_row + local * PB + i] - got_at
                        r1, c1, f1 = place_of(own_row, own_col)
                        r2, c2, f2 = place_of(got_row, got_col)
                        value = f_buf[at, pl.ds(i * MB, MB), here]
                        value += own_buf[n, r1, c1].astype(F32) * f1
                        value += got_buf[n, r2, c2].astype(F32) * f2
                        o_buf[at, pl.ds(i * MB, MB), here] = value.astype(BF16)
                        if j < tiles:
                            f_buf[at, pl.ds(i * MB, MB), here] = value
                for copy in stores[at]:
                    copy.start()
        for group in stores:
            for copy in group:
                copy.wait()

    outs = pl.pallas_call(
        kernel,
        out_shape=[jax.ShapeDtypeStruct((W, CH), BF16)] * total
        + [jax.ShapeDtypeStruct((W, W), F32)] * exacts,
        in_specs=[SMEM, HBM, HBM, HBM],
        out_specs=[HBM] * (total + exacts),
        scratch_shapes=[
            pltpu.VMEM((len(panels), W, columns), BF16),
            pltpu.VMEM((len(panels), W, columns), BF16),
            pltpu.VMEM((total, W, CH), F32),
            pltpu.VMEM((total, W, CH), BF16),
            pltpu.SemaphoreType.DMA((4 + 3 * total,)),
        ],
        compiler_params=params(FULL_MIB),
        cost_estimate=pl.CostEstimate(flops=0, bytes_accessed=32 * MIB, transcendentals=0),
        name="pivot_chunks",
    )(plan, front_matrix, child_blocks, got_rows)
    return [outs[n * count : (n + 1) * count] for n in range(len(panels))], outs[total:]


def first_columns(sz, plan, front_matrix, child_blocks, got_cols):
    def kernel(plan_ref, front_ref, own_ref, got_ref, out_ref):
        r = pl.program_id(0)
        for i in range(PB):
            own_row = plan_ref[sz.own_row + r * PB + i]
            got_row = plan_ref[sz.got_row + r * PB + i]
            for q in range(PB):
                r1, c1, f1 = place_of(own_row, plan_ref[sz.own_col + q])
                r2, c2, f2 = place_of(got_row, plan_ref[sz.got_col + q])
                here = (pl.ds(i * MB, MB), pl.ds(q * MB, MB))
                value = front_ref[0, here[0], here[1]] + own_ref[r1, c1].astype(F32) * f1
                value += got_ref[r2, c2].astype(F32) * f2
                out_ref[here] = value.astype(BF16)

    return pl.pallas_call(
        kernel,
        out_shape=jax.ShapeDtypeStruct((sz.local_rows, W), BF16),
        grid_spec=pltpu.PrefetchScalarGridSpec(
            num_scalar_prefetch=1,
            grid=(sz.row_blocks,),
            in_specs=[
                pl.BlockSpec((1, W, W), lambda r, plan: (0, r, 0)),
                pl.BlockSpec((None, None, sz.child_rows, W), lambda r, plan: (0, 0, 0, 0)),
                pl.BlockSpec((sz.child_rows, W), lambda r, plan: (0, 0)),
            ],
            out_specs=pl.BlockSpec((W, W), lambda r, plan: (r, 0)),
        ),
        compiler_params=params(FULL_MIB),
        cost_estimate=pl.CostEstimate(flops=0, bytes_accessed=32 * MIB, transcendentals=0),
        name="first_columns",
    )(plan, front_matrix, child_blocks, got_cols)


def inject(flag, rows, received):
    def kernel(flag_ref, rows_ref, received_ref, out_ref, held_ref, sems):
        @pl.when(flag_ref[0] == 1)
        def _():
            for n, (source, target) in enumerate(((rows_ref, held_ref), (held_ref, out_ref))):
                copy = pltpu.make_async_copy(source, target, sems.at[n])
                copy.start()
                copy.wait()

    return pl.pallas_call(
        kernel,
        out_shape=jax.ShapeDtypeStruct(received.shape, BF16),
        in_specs=[SMEM, HBM, HBM],
        out_specs=HBM,
        scratch_shapes=[pltpu.VMEM(received.shape, BF16), pltpu.SemaphoreType.DMA((2,))],
        input_output_aliases={2: 0},
        compiler_params=params(VMEM_MIB),
        name="inject",
    )(flag, rows, received)


def gather_tiles(sz, plan, passed):
    count = len(passed[0])

    def kernel(plan_ref, *refs):
        sources = (refs[:count], refs[count : 2 * count])
        out_ref, sems = refs[2 * count :]
        for p in range(2):
            for d in range(sz.rows):

                @pl.when(plan_ref[DIST + p] == d)
                def _():
                    for t in range(TILE_CHUNKS):
                        pltpu.make_async_copy(
                            sources[p][t + d], out_ref.at[p, t], sems.at[p, t]
                        ).start()

        for p in range(2):
            for t in range(TILE_CHUNKS):
                pltpu.make_async_copy(sources[p][t], out_ref.at[p, t], sems.at[p, t]).wait()

    return pl.pallas_call(
        kernel,
        out_shape=jax.ShapeDtypeStruct((2, TILE_CHUNKS, W, CH), BF16),
        in_specs=[SMEM] + [HBM] * (2 * count),
        out_specs=VMEM,
        scratch_shapes=[pltpu.SemaphoreType.DMA((2, TILE_CHUNKS))],
        compiler_params=params(VMEM_MIB),
        name="gather_tiles",
    )(plan, *passed[0], *passed[1])


def split(value):
    high = value.astype(BF16)
    return high, (value - high.astype(F32)).astype(BF16)


def product_of(a, b):
    dot = functools.partial(jnp.dot, preferred_element_type=F32)
    return dot(a[0], b[0]) + (dot(a[0], b[1]) + dot(a[1], b[0]))


def invert(block):
    rows = lax.broadcasted_iota(jnp.int32, (W, W), 0)
    cols = lax.broadcasted_iota(jnp.int32, (W, W), 1)
    on_diagonal = rows == cols
    diagonal = jnp.where(on_diagonal, block, 0.0)
    down = 1.0 / jnp.sum(diagonal, axis=1, keepdims=True)
    across = 1.0 / jnp.sum(diagonal, axis=0, keepdims=True)
    first = jnp.where(on_diagonal, 2.0 * down, 0.0) - down * block * across
    halves = split(first)
    return 2.0 * first - product_of(halves, split(product_of(split(block), halves)))


def tiles_of(plan_ref, mine_ref, other_ref, col, p):
    flip = plan_ref[FLIP] == 1 - col
    pair = [jnp.where(flip, other_ref[p, t], mine_ref[p, t]) for t in range(TILE_CHUNKS)]
    return jnp.concatenate(pair, axis=1)


def first_inverse(plan, mine, other, exact):
    def kernel(plan_ref, mine_ref, other_ref, exact_ref, x_ref, h_ref, l_ref):
        here = jnp.logical_and(plan_ref[OWNS] == 1, plan_ref[COL] == 0)
        tile = tiles_of(plan_ref, mine_ref, other_ref, 0, 0).astype(F32)
        x = invert(jnp.where(here, exact_ref[...], tile))
        x_ref[...] = x
        h_ref[...] = x.astype(BF16)
        tile = tiles_of(plan_ref, mine_ref, other_ref, 0, 1)
        l_ref[...] = jnp.dot(tile, h_ref[...], preferred_element_type=F32).astype(BF16)

    return pl.pallas_call(
        kernel,
        out_shape=[jax.ShapeDtypeStruct((W, W), t) for t in (F32, BF16, BF16)],
        grid=(1,),
        in_specs=[SMEM] + [TILES_SPEC] * 2 + [TILE_SPEC] * 1,
        out_specs=[TILE_SPEC] * 3,
        compiler_params=params(VMEM_MIB),
        cost_estimate=pl.CostEstimate(flops=1 << 32, bytes_accessed=4 * MIB, transcendentals=0),
        name="first_inverse",
    )(plan, mine, other, exact)


def second_inverse(plan, mine, other, exact, lower_1):
    def kernel(plan_ref, mine_ref, other_ref, exact_ref, l_ref, x_ref, h_ref, u_ref):
        here = jnp.logical_and(plan_ref[OWNS + 1] == 1, plan_ref[COL] == 1)
        u_ref[...] = tiles_of(plan_ref, mine_ref, other_ref, 1, 0)
        tile = tiles_of(plan_ref, mine_ref, other_ref, 1, 1).astype(F32)
        block = jnp.where(here, exact_ref[...], tile)
        x = invert(block - jnp.dot(l_ref[...], u_ref[...], preferred_element_type=F32))
        x_ref[...] = x
        h_ref[...] = x.astype(BF16)

    return pl.pallas_call(
        kernel,
        out_shape=[jax.ShapeDtypeStruct((W, W), t) for t in (F32, BF16, BF16)],
        grid=(1,),
        in_specs=[SMEM] + [TILES_SPEC] * 2 + [TILE_SPEC] * 2,
        out_specs=[TILE_SPEC] * 3,
        compiler_params=params(VMEM_MIB),
        cost_estimate=pl.CostEstimate(flops=1 << 32, bytes_accessed=4 * MIB, transcendentals=0),
        name="second_inverse",
    )(plan, mine, other, exact, lower_1)


def is_pivot(plan_ref, panel, r):
    return jnp.logical_and(plan_ref[OWNS + panel] == 1, plan_ref[LOCAL + panel] == r)


def multipliers(sz, plan, mine, other, half_0, half_1, upper, part):
    steps = sz.row_blocks // PARTS

    def kernel(plan_ref, mine_ref, other_ref, h0_ref, h1_ref, u_ref, out_ref):
        r = pl.program_id(0) + part * steps
        flip = plan_ref[FLIP] == 1
        keep_0 = 1.0 - is_pivot(plan_ref, 0, r).astype(F32)
        keep_1 = keep_0 * (1.0 - is_pivot(plan_ref, 1, r).astype(F32))
        first = jnp.where(flip, other_ref[...], mine_ref[...])
        lower_0 = jnp.dot(first, h0_ref[...], preferred_element_type=F32) * keep_0
        lower_0 = lower_0.astype(BF16)
        column = jnp.where(flip, mine_ref[...], other_ref[...]).astype(F32)
        column -= jnp.dot(lower_0, u_ref[...], preferred_element_type=F32)
        lower_1 = jnp.dot(column.astype(BF16), h1_ref[...], preferred_element_type=F32) * keep_1
        out_ref[:, :W] = lower_0
        out_ref[:, W:] = lower_1.astype(BF16)

    rows = pl.BlockSpec((W, W), lambda r, plan: (r + part * steps, 0))
    return pl.pallas_call(
        kernel,
        out_shape=jax.ShapeDtypeStruct((steps * W, 2 * W), BF16),
        grid_spec=pltpu.PrefetchScalarGridSpec(
            num_scalar_prefetch=1,
            grid=(steps,),
            in_specs=[rows, rows, VMEM, VMEM, VMEM],
            out_specs=pl.BlockSpec((W, 2 * W), lambda r, plan: (r, 0)),
        ),
        compiler_params=params(VMEM_MIB),
        cost_estimate=pl.CostEstimate(
            flops=6 * steps * W * W * W, bytes_accessed=5 * MIB, transcendentals=0
        ),
        name="multipliers",
    )(plan, mine, other, half_0, half_1, upper)


def tie(value, *after):
    return lax.optimization_barrier((value, *after))[0]


def update(
    sz, plan, chunk, count, front_matrix, child_blocks, partner, lower, lower_1, passed, exact, out
):
    special = chunk == 0
    width = count * CH
    per = width // MB
    start = chunk * CH // MB
    blocks = sz.row_blocks
    columns = pl.ds(chunk * CH, width)
    span = count + sz.rows - 1

    def kernel(plan_ref, front_ref, own_ref, partner_ref, *refs):
        l_refs, low_ref, refs = refs[:PARTS], refs[PARTS], refs[PARTS + 1 :]
        sources = (refs[:span], refs[span : 2 * span])
        refs = refs[2 * span :]
        if special:
            exact_refs, refs = refs[:2], refs[2:]
        out_ref, f_buf, c_buf, x_buf, upper, raw, o_buf, sems = refs[-8:]
        targets = (upper.at[pl.ds(0, W)], raw)

        def fetch(p, c, d):
            return pltpu.make_async_copy(
                sources[p][c + d], targets[p].at[:, pl.ds(c * CH, CH)], sems.at[p * count + c]
            )

        for p in range(2):
            for d in range(sz.rows):

                @pl.when(plan_ref[DIST + p] == d)
                def _():
                    for c in range(count):
                        fetch(p, c, d).start()

        head = [fetch(p, c, 0) for p in range(2) for c in range(count)]
        children = []
        for n, (child, which, at) in enumerate(
            ((own_ref, 0, sz.own_col), (partner_ref, 1, sz.got_col))
        ):
            for q in range(per):
                b = jnp.maximum(plan_ref[at + start + q], 0)
                b = pl.ds(pl.multiple_of(b * MB, MB), MB)
                children.append(
                    pltpu.make_async_copy(
                        child.at[0, which, :, b], c_buf.at[n, q], sems.at[2 * count + n * per + q]
                    )
                )
                children[-1].start()
        base = 2 * count + 2 * per
        if special:
            for p in range(2):
                children.append(
                    pltpu.make_async_copy(
                        exact_refs[p].at[:, columns], x_buf.at[p], sems.at[base + p]
                    )
                )
                children[-1].start()
        base += 2
        loads, stores = [], []
        for r in range(blocks):
            rows = pl.ds(r * W, W)
            loads.append(
                pltpu.make_async_copy(
                    front_ref.at[0, rows, columns], f_buf.at[rows], sems.at[base + 2 * r]
                )
            )
            stores.append(
                pltpu.make_async_copy(
                    o_buf.at[rows], out_ref.at[0, rows, columns], sems.at[base + 2 * r + 1]
                )
            )
            loads[-1].start()
        for copy in head:
            copy.wait()
        product = jnp.dot(low_ref[...], upper[:W], preferred_element_type=F32)
        upper[W:] = (raw[...].astype(F32) - product).astype(BF16)
        for r in range(blocks):
            l_ref, l_rows = l_refs[r // (blocks // PARTS)], pl.ds(r % (blocks // PARTS) * W, W)
            product = jnp.dot(l_ref[l_rows], upper[...], preferred_element_type=F32)
            for copy in children if r == 0 else ():
                copy.wait()
            loads[r].wait()
            for q in range(per):
                here = pl.ds(q * MB, MB)
                own_col = plan_ref[sz.own_col + start + q]
                got_col = plan_ref[sz.got_col + start + q]
                for i in range(PB):
                    rows = pl.ds(r * W + i * MB, MB)
                    r1, _, f1 = place_of(plan_ref[sz.own_row + r * PB + i], own_col)
                    r2, _, f2 = place_of(plan_ref[sz.got_row + r * PB + i], got_col)
                    value = f_buf[rows, here] + c_buf[0, q, r1, :].astype(F32) * f1
                    value += c_buf[1, q, r2, :].astype(F32) * f2
                    value -= product[i * MB : (i + 1) * MB, q * MB : (q + 1) * MB]
                    o_buf[rows, here] = value
            if special:
                col = plan_ref[COL]
                first, second = is_pivot(plan_ref, 0, r), is_pivot(plan_ref, 1, r)
                rows = pl.ds(r * W, W)

                @pl.when(jnp.logical_and(col == 0, first))
                def _():
                    o_buf[rows] = x_buf[0]

                @pl.when(jnp.logical_and(col == 0, jnp.logical_not(first)))
                def _():
                    o_buf[rows] = l_ref[l_rows, columns].astype(F32)

                @pl.when(jnp.logical_and(col == 1, second))
                def _():
                    o_buf[rows] = x_buf[1]

                @pl.when(jnp.logical_and(col == 1, jnp.logical_not(jnp.logical_or(first, second))))
                def _():
                    o_buf[rows] = l_ref[l_rows, pl.ds(W, width)].astype(F32)

            stores[r].start()
        for copy in stores:
            copy.wait()

    operands = [plan, front_matrix, child_blocks, partner, *lower, lower_1]
    operands += list(passed[0]) + list(passed[1])
    if special:
        operands += list(exact)
    aliases = {}
    if out is not None:
        aliases = {len(operands): 0}
        operands.append(out)
    return pl.pallas_call(
        kernel,
        out_shape=jax.ShapeDtypeStruct(front_matrix.shape, F32),
        in_specs=[SMEM] + [HBM] * 3 + [VMEM] * (PARTS + 1) + [HBM] * (len(operands) - PARTS - 5),
        out_specs=HBM,
        scratch_shapes=[
            pltpu.VMEM((sz.local_rows, width), F32),
            pltpu.VMEM((2, per, sz.child_rows, MB), BF16),
            pltpu.VMEM((2, W, width), F32),
            pltpu.VMEM((2 * W, width), BF16),
            pltpu.VMEM((W, width), BF16),
            pltpu.VMEM((sz.local_rows, width), F32),
            pltpu.SemaphoreType.DMA((2 * count + 2 * per + 2 + 2 * blocks,)),
        ],
        input_output_aliases=aliases,
        compiler_params=params(VMEM_MIB),
        cost_estimate=pl.CostEstimate(
            flops=4 * sz.local_rows * W * width, bytes_accessed=8 * count * MIB, transcendentals=0
        ),
        name="update",
    )(*operands)


def tie(value, *after):
    return lax.optimization_barrier((value, *after))[0]


def from_first_two(cols, col, mine):
    if cols == 2:
        return mine, lax.ppermute(mine, "col", [(0, 1), (1, 0)])
    zero = jnp.zeros_like(mine)
    return tuple(lax.psum(jnp.where(col == c, mine, zero), "col") for c in range(2))


def body(rows, cols, front_matrix, child_blocks, child_maps, pivot_rows):
    sz = Sizes(rows, cols, front_matrix.shape[1:], child_blocks.shape[2:])
    front_count = lax.axis_size("front")
    swap = [(f, f ^ 1) for f in range(front_count)]
    order = [0] + list(range(1, rows, 2)) + sorted(range(2, rows, 2), reverse=True)
    ring = [(order[i], order[(i + 1) % rows]) for i in range(rows)]
    front, row, col = (lax.axis_index(a).astype(jnp.int32) for a in ("front", "row", "col"))
    ids = jnp.stack([front, row, col])
    plan = make_plan(sz, ids, child_maps, pivot_rows)
    pivots = lax.dynamic_index_in_dim(pivot_rows, front, 0, keepdims=False)
    flags = [(pivots[k : k + 1] // sz.row_blocks == row).astype(jnp.int32) for k in range(2)]

    early = min(EARLY_CHUNKS, sz.chunks)
    sent = cut_rows(sz, plan, child_blocks, min(early * CH, sz.child_cols))
    got = lax.ppermute(sent, "front", swap)
    panel_rows, (exact_0, exact_1) = pivot_chunks(
        sz, plan, front_matrix, child_blocks, got, (0, 1), 0, early
    )
    first = panel_rows[0][0]
    got_cols = lax.ppermute(cut_cols(sz, tie(child_blocks, got)), "front", swap)
    if early < sz.chunks:
        sent = cut_rows(sz, plan, tie(child_blocks, first), sz.child_cols)
        got = lax.ppermute(sent, "front", swap)

    steps = sz.chunks + rows - 2
    columns_step = 1
    tiles_step = min(rows, steps - 1)
    settled_step = tiles_step + 2
    algebra_step = tiles_step + 4
    passed = ([], [])
    held = [panel_rows[0][0], panel_rows[1][0]]
    mine = tiles = columns = partner = lower_1 = half = upper = lower = out = None
    exact, waits = [], []

    def inverses():
        nonlocal lower_1, half, upper
        x_0, half_0, lower_1 = first_inverse(plan, *tiles, exact_0)
        x_1, half_1, upper = second_inverse(plan, *tiles, exact_1, lower_1)
        half = (half_0, half_1)
        exact.extend((x_0, x_1))
        return half_1

    def all_multipliers():
        nonlocal lower
        lower = [multipliers(sz, plan, *columns, *half, upper, n) for n in range(PARTS)]
        return lower[-1]

    def updates(chunk, count):
        nonlocal out
        at = [passed[p][chunk : chunk + count + rows - 1] for p in range(2)]
        out = update(
            sz, plan, chunk, count, front_matrix, child_blocks, partner, lower, lower_1, at, exact, out
        )
        return out

    todo = [(0, inverses), (0, all_multipliers)]
    chunk = 0
    while chunk < sz.chunks:
        count = TILE_CHUNKS if chunk + TILE_CHUNKS <= sz.chunks - TILE_CHUNKS else 1
        todo.append((chunk + count + rows - 2, functools.partial(updates, chunk, count)))
        chunk += count

    after = ()
    for s in range(steps):
        for k in range(2):
            if s and s < sz.chunks:
                held[k] = inject(flags[k], panel_rows[k][s], tie(held[k], *after))
            elif s:
                held[k] = tie(held[k], *after)
            after = ()
            passed[k].append(held[k])
            held[k] = lax.ppermute(held[k], "row", ring)
        last = passed[1][-1]
        if s == columns_step:
            mine = first_columns(sz, plan, front_matrix, child_blocks, tie(got_cols, last))
            partner = lax.ppermute(tie(child_blocks, mine), "front", swap)
            columns = from_first_two(cols, col, mine)
            after = (mine,)
        if early < sz.chunks and s in (columns_step + 1, columns_step + 2):
            k = s - columns_step - 1
            (more,), _ = pivot_chunks(
                sz, plan, front_matrix, child_blocks, tie(got, last), (k,), early, sz.chunks - early
            )
            panel_rows[k] = panel_rows[k] + more
            after = (more[0],)
        if s == tiles_step:
            mine = gather_tiles(sz, plan, [passed[p][: TILE_CHUNKS + rows - 1] for p in range(2)])
            tiles = from_first_two(cols, col, mine)
            after = (mine,)
        if s == settled_step:
            columns = tie(columns, last)
            after = (columns[1],)
        if s == algebra_step:
            tiles = tie(tiles, last)
        if s >= algebra_step and todo[0][0] <= s:
            after = (todo.pop(0)[1](),)
    for k in range(2):
        passed[k].append(held[k])
    for _, piece in todo:
        piece()
    return out


def solution(mesh):
    in_specs = (P("front", "row", "col"), P("front", None, "row", "col"), P(), P())
    out_specs = P("front", "row", "col")
    step = functools.partial(body, mesh.shape["row"], mesh.shape["col"])
    return jax.shard_map(step, mesh=mesh, in_specs=in_specs, out_specs=out_specs, check_vma=False)
```

```python
import functools

import jax
import jax.numpy as jnp
from jax import lax
from jax.experimental import pallas as pl
from jax.experimental.pallas import tpu as pltpu
from jax.sharding import PartitionSpec as P

W = 512
MB = 128
CH = 256
PB = W // MB
TILE_CHUNKS = W // CH
EARLY_CHUNKS = 6
PARTS = 2
HBM = pl.BlockSpec(memory_space=pltpu.HBM)
SMEM = pl.BlockSpec(memory_space=pltpu.SMEM)
TILE_SPEC = pl.BlockSpec((W, W), lambda i: (0, 0))
TILES_SPEC = pl.BlockSpec((2, TILE_CHUNKS, W, CH), lambda i: (0, 0, 0, 0))
F32 = jnp.float32
BF16 = jnp.bfloat16
MIB = 1 << 20
VMEM_MIB = 48
FULL_MIB = 60
VMEM = pl.BlockSpec(memory_space=pltpu.VMEM)

OWNS, DIST, LOCAL, OWN_AT, GOT_AT, SEND_AT, COL, FLIP, LISTS = 0, 2, 4, 6, 8, 10, 12, 13, 16


class Sizes:
    def __init__(self, rows, cols, front, child):
        self.rows, self.cols = rows, cols
        self.local_rows, self.local_cols = front
        self.child_rows, self.child_cols = child
        self.row_blocks = self.local_rows // W
        self.chunks = self.local_cols // CH
        self.map_rows, self.map_cols = self.local_rows // MB, self.local_cols // MB
        self.own_row = LISTS
        self.got_row = self.own_row + self.map_rows
        self.own_col = self.got_row + self.map_rows
        self.got_col = self.own_col + self.map_cols
        self.plan = self.got_col + self.map_cols


def params(mib):
    return pltpu.CompilerParams(vmem_limit_bytes=mib * MIB)


def make_plan(sz, ids, child_maps, pivot_rows):
    child_row_blocks = sz.child_rows // MB
    child_col_blocks = sz.child_cols // MB

    def place(z):
        return jnp.where(z % 2 == 1, (z + 1) // 2, jnp.where(z == 0, 0, sz.rows - z // 2))

    def kernel(ids_ref, maps_ref, order_ref, out_ref):
        front, row, col = ids_ref[0], ids_ref[1], ids_ref[2]
        partner = jnp.bitwise_xor(front, 1)
        for i in range(FLIP + 1, LISTS):
            out_ref[i] = 0
        out_ref[COL] = col
        out_ref[FLIP] = col if sz.cols == 2 else jnp.int32(0)

        def start(f, s, local):
            count = jnp.int32(0)
            for b in range(child_row_blocks):
                at = maps_ref[f, s, row * child_row_blocks + b] - row * sz.map_rows
                count += (at < local * PB).astype(jnp.int32)
            return jnp.minimum(count, child_row_blocks - PB)

        for p in range(2):
            pivot = order_ref[front, p]
            owner = pivot // sz.row_blocks
            local = pivot - owner * sz.row_blocks
            other = order_ref[partner, p] % sz.row_blocks
            out_ref[OWNS + p] = (owner == row).astype(jnp.int32)
            out_ref[DIST + p] = (place(row) - place(owner) + sz.rows) % sz.rows
            out_ref[LOCAL + p] = local
            out_ref[OWN_AT + p] = start(front, 0, local)
            out_ref[GOT_AT + p] = start(partner, 1, local)
            out_ref[SEND_AT + p] = start(front, 1, other)
        for f, s, row_list, col_list in (
            (front, 0, sz.own_row, sz.own_col),
            (partner, 1, sz.got_row, sz.got_col),
        ):
            for i in range(sz.map_rows):
                out_ref[row_list + i] = -1
            for i in range(sz.map_cols):
                out_ref[col_list + i] = -1
            for b in range(child_row_blocks):
                at = maps_ref[f, s, row * child_row_blocks + b] - row * sz.map_rows
                out_ref[row_list + at] = b
            for b in range(child_col_blocks):
                at = maps_ref[f, s, col * child_col_blocks + b] - col * sz.map_cols
                out_ref[col_list + at] = b

    return pl.pallas_call(
        kernel,
        out_shape=jax.ShapeDtypeStruct((sz.plan,), jnp.int32),
        in_specs=[SMEM] * 3,
        out_specs=SMEM,
        compiler_params=params(FULL_MIB),
        name="plan",
    )(ids, child_maps, pivot_rows)


def cut_rows(sz, plan, child_blocks, columns):
    def kernel(plan_ref, child_ref, out_ref, sems):
        copies = []
        for p in range(2):
            at = pl.multiple_of(plan_ref[SEND_AT + p] * MB, MB)
            source = child_ref.at[0, 1, pl.ds(at, W), pl.ds(0, columns)]
            copies.append(pltpu.make_async_copy(source, out_ref.at[p], sems.at[p]))
            copies[-1].start()
        for copy in copies:
            copy.wait()

    return pl.pallas_call(
        kernel,
        out_shape=jax.ShapeDtypeStruct((2, W, columns), BF16),
        in_specs=[SMEM, HBM],
        out_specs=VMEM,
        scratch_shapes=[pltpu.SemaphoreType.DMA((2,))],
        compiler_params=params(VMEM_MIB),
        cost_estimate=pl.CostEstimate(flops=0, bytes_accessed=10 * MIB, transcendentals=0),
        name="cut_rows",
    )(plan, child_blocks)


def cut_cols(sz, child_blocks):
    def kernel(child_ref, out_ref, sem):
        copy = pltpu.make_async_copy(child_ref.at[0, 1, :, pl.ds(0, W)], out_ref, sem)
        copy.start()
        copy.wait()

    return pl.pallas_call(
        kernel,
        out_shape=jax.ShapeDtypeStruct((sz.child_rows, W), BF16),
        in_specs=[HBM],
        out_specs=VMEM,
        scratch_shapes=[pltpu.SemaphoreType.DMA],
        compiler_params=params(FULL_MIB),
        name="cut_cols",
    )(child_blocks)


def place_of(row, col):
    there = jnp.logical_and(row >= 0, col >= 0).astype(F32)
    row_at = pl.multiple_of(jnp.maximum(row, 0) * MB, MB)
    col_at = pl.multiple_of(jnp.maximum(col, 0) * MB, MB)
    return pl.ds(row_at, MB), pl.ds(col_at, MB), there


def pivot_chunks(sz, plan, front_matrix, child_blocks, got_rows, panels, first, count):
    whole = got_rows.ndim == 4
    columns = got_rows.shape[-1]
    tiles = TILE_CHUNKS if first == 0 else 0
    total = len(panels) * count
    exacts = len(panels) if tiles else 0

    def kernel(plan_ref, front_ref, child_ref, got_ref, *refs):
        rows_refs, exact_refs = refs[:total], refs[total : total + exacts]
        own_buf, got_buf, f_buf, o_buf, sems = refs[total + exacts :]
        children, loads, stores = [], [], []
        for n, p in enumerate(panels):
            at = pl.multiple_of(plan_ref[OWN_AT + p] * MB, MB)
            source = child_ref.at[0, 0, pl.ds(at, W), pl.ds(0, columns)]
            children.append(pltpu.make_async_copy(source, own_buf.at[n], sems.at[2 * n]))
            at = pl.multiple_of(plan_ref[GOT_AT + p] * MB, MB)
            source = got_ref.at[0, 1, pl.ds(at, W)] if whole else got_ref.at[p]
            children.append(pltpu.make_async_copy(source, got_buf.at[n], sems.at[2 * n + 1]))
        for copy in children:
            copy.start()
        for n, p in enumerate(panels):
            rows = pl.ds(pl.multiple_of(plan_ref[LOCAL + p] * W, W), W)
            for j in range(count):
                at = n * count + j
                base = 4 + 3 * at
                source = front_ref.at[0, rows, pl.ds((first + j) * CH, CH)]
                loads.append(pltpu.make_async_copy(source, f_buf.at[at], sems.at[base]))
                loads[-1].start()
                stores.append(
                    [pltpu.make_async_copy(o_buf.at[at], rows_refs[at], sems.at[base + 1])]
                )
                if j < tiles:
                    target = exact_refs[n].at[:, pl.ds(j * CH, CH)]
                    stores[-1].append(
                        pltpu.make_async_copy(f_buf.at[at], target, sems.at[base + 2])
                    )
        for copy in children:
            copy.wait()
        for n, p in enumerate(panels):
            own_at, got_at = plan_ref[OWN_AT + p], plan_ref[GOT_AT + p]
            local = plan_ref[LOCAL + p]
            for j in range(count):
                at = n * count + j
                loads[at].wait()
                for q in range(CH // MB):
                    here = pl.ds(q * MB, MB)
                    own_col = plan_ref[sz.own_col + (first + j) * (CH // MB) + q]
                    got_col = plan_ref[sz.got_col + (first + j) * (CH // MB) + q]
                    for i in range(PB):
                        own_row = plan_ref[sz.own_row + local * PB + i] - own_at
                        got_row = plan_ref[sz.got_row + local * PB + i] - got_at
                        r1, c1, f1 = place_of(own_row, own_col)
                        r2, c2, f2 = place_of(got_row, got_col)
                        value = f_buf[at, pl.ds(i * MB, MB), here]
                        value += own_buf[n, r1, c1].astype(F32) * f1
                        value += got_buf[n, r2, c2].astype(F32) * f2
                        o_buf[at, pl.ds(i * MB, MB), here] = value.astype(BF16)
                        if j < tiles:
                            f_buf[at, pl.ds(i * MB, MB), here] = value
                for copy in stores[at]:
                    copy.start()
        for group in stores:
            for copy in group:
                copy.wait()

    outs = pl.pallas_call(
        kernel,
        out_shape=[jax.ShapeDtypeStruct((W, CH), BF16)] * total
        + [jax.ShapeDtypeStruct((W, W), F32)] * exacts,
        in_specs=[SMEM, HBM, HBM, HBM],
        out_specs=[HBM] * (total + exacts),
        scratch_shapes=[
            pltpu.VMEM((len(panels), W, columns), BF16),
            pltpu.VMEM((len(panels), W, columns), BF16),
            pltpu.VMEM((total, W, CH), F32),
            pltpu.VMEM((total, W, CH), BF16),
            pltpu.SemaphoreType.DMA((4 + 3 * total,)),
        ],
        compiler_params=params(FULL_MIB),
        cost_estimate=pl.CostEstimate(flops=0, bytes_accessed=12 * MIB, transcendentals=0),
        name="pivot_chunks",
    )(plan, front_matrix, child_blocks, got_rows)
    return [outs[n * count : (n + 1) * count] for n in range(len(panels))], outs[total:]


def first_columns(sz, plan, front_matrix, child_blocks, got_cols):
    def kernel(plan_ref, front_ref, own_ref, got_ref, out_ref):
        r = pl.program_id(0)
        for i in range(PB):
            own_row = plan_ref[sz.own_row + r * PB + i]
            got_row = plan_ref[sz.got_row + r * PB + i]
            for q in range(PB):
                r1, c1, f1 = place_of(own_row, plan_ref[sz.own_col + q])
                r2, c2, f2 = place_of(got_row, plan_ref[sz.got_col + q])
                here = (pl.ds(i * MB, MB), pl.ds(q * MB, MB))
                value = front_ref[0, here[0], here[1]] + own_ref[r1, c1].astype(F32) * f1
                value += got_ref[r2, c2].astype(F32) * f2
                out_ref[here] = value.astype(BF16)

    return pl.pallas_call(
        kernel,
        out_shape=jax.ShapeDtypeStruct((sz.local_rows, W), BF16),
        grid_spec=pltpu.PrefetchScalarGridSpec(
            num_scalar_prefetch=1,
            grid=(sz.row_blocks,),
            in_specs=[
                pl.BlockSpec((1, W, W), lambda r, plan: (0, r, 0)),
                pl.BlockSpec((None, None, sz.child_rows, W), lambda r, plan: (0, 0, 0, 0)),
                pl.BlockSpec((sz.child_rows, W), lambda r, plan: (0, 0)),
            ],
            out_specs=pl.BlockSpec((W, W), lambda r, plan: (r, 0)),
        ),
        compiler_params=params(FULL_MIB),
        cost_estimate=pl.CostEstimate(flops=0, bytes_accessed=12 * MIB, transcendentals=0),
        name="first_columns",
    )(plan, front_matrix, child_blocks, got_cols)


def inject(flag, rows, received):
    def kernel(flag_ref, rows_ref, received_ref, out_ref, held_ref, sems):
        @pl.when(flag_ref[0] == 1)
        def _():
            for n, (source, target) in enumerate(((rows_ref, held_ref), (held_ref, out_ref))):
                copy = pltpu.make_async_copy(source, target, sems.at[n])
                copy.start()
                copy.wait()

    return pl.pallas_call(
        kernel,
        out_shape=jax.ShapeDtypeStruct(received.shape, BF16),
        in_specs=[SMEM, HBM, HBM],
        out_specs=HBM,
        scratch_shapes=[pltpu.VMEM(received.shape, BF16), pltpu.SemaphoreType.DMA((2,))],
        input_output_aliases={2: 0},
        compiler_params=params(VMEM_MIB),
        name="inject",
    )(flag, rows, received)


def gather_tiles(sz, plan, passed):
    count = len(passed[0])

    def kernel(plan_ref, *refs):
        sources = (refs[:count], refs[count : 2 * count])
        out_ref, sems = refs[2 * count :]
        for p in range(2):
            for d in range(sz.rows):

                @pl.when(plan_ref[DIST + p] == d)
                def _():
                    for t in range(TILE_CHUNKS):
                        pltpu.make_async_copy(
                            sources[p][t + d], out_ref.at[p, t], sems.at[p, t]
                        ).start()

        for p in range(2):
            for t in range(TILE_CHUNKS):
                pltpu.make_async_copy(sources[p][t], out_ref.at[p, t], sems.at[p, t]).wait()

    return pl.pallas_call(
        kernel,
        out_shape=jax.ShapeDtypeStruct((2, TILE_CHUNKS, W, CH), BF16),
        in_specs=[SMEM] + [HBM] * (2 * count),
        out_specs=VMEM,
        scratch_shapes=[pltpu.SemaphoreType.DMA((2, TILE_CHUNKS))],
        compiler_params=params(FULL_MIB),
        name="gather_tiles",
    )(plan, *passed[0], *passed[1])


def split(value):
    high = value.astype(BF16)
    return high, (value - high.astype(F32)).astype(BF16)


def product_of(a, b):
    dot = functools.partial(jnp.dot, preferred_element_type=F32)
    return dot(a[0], b[0]) + (dot(a[0], b[1]) + dot(a[1], b[0]))


def invert(block):
    rows = lax.broadcasted_iota(jnp.int32, (W, W), 0)
    cols = lax.broadcasted_iota(jnp.int32, (W, W), 1)
    on_diagonal = rows == cols
    diagonal = jnp.where(on_diagonal, block, 0.0)
    down = 1.0 / jnp.sum(diagonal, axis=1, keepdims=True)
    across = 1.0 / jnp.sum(diagonal, axis=0, keepdims=True)
    first = jnp.where(on_diagonal, 2.0 * down, 0.0) - down * block * across
    halves = split(first)
    return 2.0 * first - product_of(halves, split(product_of(split(block), halves)))


def tiles_of(plan_ref, mine_ref, other_ref, col, p):
    flip = plan_ref[FLIP] == 1 - col
    pair = [jnp.where(flip, other_ref[p, t], mine_ref[p, t]) for t in range(TILE_CHUNKS)]
    return jnp.concatenate(pair, axis=1)


def first_inverse(plan, mine, other, exact):
    def kernel(plan_ref, mine_ref, other_ref, exact_ref, x_ref, h_ref, l_ref):
        here = jnp.logical_and(plan_ref[OWNS] == 1, plan_ref[COL] == 0)
        tile = tiles_of(plan_ref, mine_ref, other_ref, 0, 0).astype(F32)
        x = invert(jnp.where(here, exact_ref[...], tile))
        x_ref[...] = x
        h_ref[...] = x.astype(BF16)
        tile = tiles_of(plan_ref, mine_ref, other_ref, 0, 1)
        l_ref[...] = jnp.dot(tile, h_ref[...], preferred_element_type=F32).astype(BF16)

    return pl.pallas_call(
        kernel,
        out_shape=[jax.ShapeDtypeStruct((W, W), t) for t in (F32, BF16, BF16)],
        grid=(1,),
        in_specs=[SMEM] + [TILES_SPEC] * 2 + [TILE_SPEC] * 1,
        out_specs=[TILE_SPEC] * 3,
        compiler_params=params(VMEM_MIB),
        cost_estimate=pl.CostEstimate(flops=1 << 32, bytes_accessed=4 * MIB, transcendentals=0),
        name="first_inverse",
    )(plan, mine, other, exact)


def second_inverse(plan, mine, other, exact, lower_1):
    def kernel(plan_ref, mine_ref, other_ref, exact_ref, l_ref, x_ref, h_ref, u_ref):
        here = jnp.logical_and(plan_ref[OWNS + 1] == 1, plan_ref[COL] == 1)
        u_ref[...] = tiles_of(plan_ref, mine_ref, other_ref, 1, 0)
        tile = tiles_of(plan_ref, mine_ref, other_ref, 1, 1).astype(F32)
        block = jnp.where(here, exact_ref[...], tile)
        x = invert(block - jnp.dot(l_ref[...], u_ref[...], preferred_element_type=F32))
        x_ref[...] = x
        h_ref[...] = x.astype(BF16)

    return pl.pallas_call(
        kernel,
        out_shape=[jax.ShapeDtypeStruct((W, W), t) for t in (F32, BF16, BF16)],
        grid=(1,),
        in_specs=[SMEM] + [TILES_SPEC] * 2 + [TILE_SPEC] * 2,
        out_specs=[TILE_SPEC] * 3,
        compiler_params=params(VMEM_MIB),
        cost_estimate=pl.CostEstimate(flops=1 << 32, bytes_accessed=4 * MIB, transcendentals=0),
        name="second_inverse",
    )(plan, mine, other, exact, lower_1)


def is_pivot(plan_ref, panel, r):
    return jnp.logical_and(plan_ref[OWNS + panel] == 1, plan_ref[LOCAL + panel] == r)


def multipliers(sz, plan, mine, other, half_0, half_1, upper, part):
    steps = sz.row_blocks // PARTS

    def kernel(plan_ref, mine_ref, other_ref, h0_ref, h1_ref, u_ref, out_ref):
        r = pl.program_id(0) + part * steps
        flip = plan_ref[FLIP] == 1
        keep_0 = 1.0 - is_pivot(plan_ref, 0, r).astype(F32)
        keep_1 = keep_0 * (1.0 - is_pivot(plan_ref, 1, r).astype(F32))
        first = jnp.where(flip, other_ref[...], mine_ref[...])
        lower_0 = jnp.dot(first, h0_ref[...], preferred_element_type=F32) * keep_0
        lower_0 = lower_0.astype(BF16)
        column = jnp.where(flip, mine_ref[...], other_ref[...]).astype(F32)
        column -= jnp.dot(lower_0, u_ref[...], preferred_element_type=F32)
        lower_1 = jnp.dot(column.astype(BF16), h1_ref[...], preferred_element_type=F32) * keep_1
        out_ref[:, :W] = lower_0
        out_ref[:, W:] = lower_1.astype(BF16)

    rows = pl.BlockSpec((W, W), lambda r, plan: (r + part * steps, 0))
    return pl.pallas_call(
        kernel,
        out_shape=jax.ShapeDtypeStruct((steps * W, 2 * W), BF16),
        grid_spec=pltpu.PrefetchScalarGridSpec(
            num_scalar_prefetch=1,
            grid=(steps,),
            in_specs=[rows, rows, VMEM, VMEM, VMEM],
            out_specs=pl.BlockSpec((W, 2 * W), lambda r, plan: (r, 0)),
        ),
        compiler_params=params(VMEM_MIB),
        cost_estimate=pl.CostEstimate(
            flops=6 * steps * W * W * W, bytes_accessed=5 * MIB, transcendentals=0
        ),
        name="multipliers",
    )(plan, mine, other, half_0, half_1, upper)


def tie(value, *after):
    return lax.optimization_barrier((value, *after))[0]


def update(
    sz, plan, chunk, count, front_matrix, child_blocks, partner, lower, lower_1, passed, exact, out
):
    special = chunk == 0
    width = count * CH
    per = width // MB
    start = chunk * CH // MB
    blocks = sz.row_blocks
    columns = pl.ds(chunk * CH, width)
    span = count + sz.rows - 1

    def kernel(plan_ref, front_ref, own_ref, partner_ref, *refs):
        l_refs, low_ref, refs = refs[:PARTS], refs[PARTS], refs[PARTS + 1 :]
        sources = (refs[:span], refs[span : 2 * span])
        refs = refs[2 * span :]
        if special:
            exact_refs, refs = refs[:2], refs[2:]
        out_ref, f_buf, c_buf, x_buf, upper, raw, o_buf, sems = refs[-8:]
        targets = (upper.at[pl.ds(0, W)], raw)

        def fetch(p, c, d):
            return pltpu.make_async_copy(
                sources[p][c + d], targets[p].at[:, pl.ds(c * CH, CH)], sems.at[p * count + c]
            )

        for p in range(2):
            for d in range(sz.rows):

                @pl.when(plan_ref[DIST + p] == d)
                def _():
                    for c in range(count):
                        fetch(p, c, d).start()

        head = [fetch(p, c, 0) for p in range(2) for c in range(count)]
        children = []
        for n, (child, which, at) in enumerate(
            ((own_ref, 0, sz.own_col), (partner_ref, 1, sz.got_col))
        ):
            for q in range(per):
                b = jnp.maximum(plan_ref[at + start + q], 0)
                b = pl.ds(pl.multiple_of(b * MB, MB), MB)
                children.append(
                    pltpu.make_async_copy(
                        child.at[0, which, :, b], c_buf.at[n, q], sems.at[2 * count + n * per + q]
                    )
                )
                children[-1].start()
        base = 2 * count + 2 * per
        if special:
            for p in range(2):
                children.append(
                    pltpu.make_async_copy(
                        exact_refs[p].at[:, columns], x_buf.at[p], sems.at[base + p]
                    )
                )
                children[-1].start()
        base += 2
        loads, stores = [], []
        for r in range(blocks):
            rows = pl.ds(r * W, W)
            loads.append(
                pltpu.make_async_copy(
                    front_ref.at[0, rows, columns], f_buf.at[rows], sems.at[base + 2 * r]
                )
            )
            stores.append(
                pltpu.make_async_copy(
                    o_buf.at[rows], out_ref.at[0, rows, columns], sems.at[base + 2 * r + 1]
                )
            )
            loads[-1].start()
        for copy in head:
            copy.wait()
        product = jnp.dot(low_ref[...], upper[:W], preferred_element_type=F32)
        upper[W:] = (raw[...].astype(F32) - product).astype(BF16)
        for r in range(blocks):
            l_ref, l_rows = l_refs[r // (blocks // PARTS)], pl.ds(r % (blocks // PARTS) * W, W)
            product = jnp.dot(l_ref[l_rows], upper[...], preferred_element_type=F32)
            for copy in children if r == 0 else ():
                copy.wait()
            loads[r].wait()
            for q in range(per):
                here = pl.ds(q * MB, MB)
                own_col = plan_ref[sz.own_col + start + q]
                got_col = plan_ref[sz.got_col + start + q]
                for i in range(PB):
                    rows = pl.ds(r * W + i * MB, MB)
                    r1, _, f1 = place_of(plan_ref[sz.own_row + r * PB + i], own_col)
                    r2, _, f2 = place_of(plan_ref[sz.got_row + r * PB + i], got_col)
                    value = f_buf[rows, here] + c_buf[0, q, r1, :].astype(F32) * f1
                    value += c_buf[1, q, r2, :].astype(F32) * f2
                    value -= product[i * MB : (i + 1) * MB, q * MB : (q + 1) * MB]
                    o_buf[rows, here] = value
            if special:
                col = plan_ref[COL]
                first, second = is_pivot(plan_ref, 0, r), is_pivot(plan_ref, 1, r)
                rows = pl.ds(r * W, W)

                @pl.when(jnp.logical_and(col == 0, first))
                def _():
                    o_buf[rows] = x_buf[0]

                @pl.when(jnp.logical_and(col == 0, jnp.logical_not(first)))
                def _():
                    o_buf[rows] = l_ref[l_rows, columns].astype(F32)

                @pl.when(jnp.logical_and(col == 1, second))
                def _():
                    o_buf[rows] = x_buf[1]

                @pl.when(jnp.logical_and(col == 1, jnp.logical_not(jnp.logical_or(first, second))))
                def _():
                    o_buf[rows] = l_ref[l_rows, pl.ds(W, width)].astype(F32)

            stores[r].start()
        for copy in stores:
            copy.wait()

    operands = [plan, front_matrix, child_blocks, partner, *lower, lower_1]
    operands += list(passed[0]) + list(passed[1])
    if special:
        operands += list(exact)
    aliases = {}
    if out is not None:
        aliases = {len(operands): 0}
        operands.append(out)
    return pl.pallas_call(
        kernel,
        out_shape=jax.ShapeDtypeStruct(front_matrix.shape, F32),
        in_specs=[SMEM] + [HBM] * 3 + [VMEM] * (PARTS + 1) + [HBM] * (len(operands) - PARTS - 5),
        out_specs=HBM,
        scratch_shapes=[
            pltpu.VMEM((sz.local_rows, width), F32),
            pltpu.VMEM((2, per, sz.child_rows, MB), BF16),
            pltpu.VMEM((2, W, width), F32),
            pltpu.VMEM((2 * W, width), BF16),
            pltpu.VMEM((W, width), BF16),
            pltpu.VMEM((sz.local_rows, width), F32),
            pltpu.SemaphoreType.DMA((2 * count + 2 * per + 2 + 2 * blocks,)),
        ],
        input_output_aliases=aliases,
        compiler_params=params(VMEM_MIB),
        cost_estimate=pl.CostEstimate(
            flops=4 * sz.local_rows * W * width, bytes_accessed=8 * count * MIB, transcendentals=0
        ),
        name="update",
    )(*operands)


def tie(value, *after):
    return lax.optimization_barrier((value, *after))[0]


def from_first_two(cols, col, mine):
    if cols == 2:
        return mine, lax.ppermute(mine, "col", [(0, 1), (1, 0)])
    zero = jnp.zeros_like(mine)
    return tuple(lax.psum(jnp.where(col == c, mine, zero), "col") for c in range(2))


def body(rows, cols, front_matrix, child_blocks, child_maps, pivot_rows):
    sz = Sizes(rows, cols, front_matrix.shape[1:], child_blocks.shape[2:])
    front_count = lax.axis_size("front")
    swap = [(f, f ^ 1) for f in range(front_count)]
    order = [0] + list(range(1, rows, 2)) + sorted(range(2, rows, 2), reverse=True)
    ring = [(order[i], order[(i + 1) % rows]) for i in range(rows)]
    front, row, col = (lax.axis_index(a).astype(jnp.int32) for a in ("front", "row", "col"))
    ids = jnp.stack([front, row, col])
    plan = make_plan(sz, ids, child_maps, pivot_rows)
    pivots = lax.dynamic_index_in_dim(pivot_rows, front, 0, keepdims=False)
    flags = [(pivots[k : k + 1] // sz.row_blocks == row).astype(jnp.int32) for k in range(2)]

    early = min(EARLY_CHUNKS, sz.chunks)
    sent = cut_rows(sz, plan, child_blocks, min(early * CH, sz.child_cols))
    got = lax.ppermute(sent, "front", swap)
    got_cols = lax.ppermute(cut_cols(sz, tie(child_blocks, sent)), "front", swap)
    panel_rows, (exact_0, exact_1) = pivot_chunks(
        sz, plan, front_matrix, child_blocks, tie(got, got_cols), (0, 1), 0, early
    )
    first = panel_rows[0][0]
    partner = lax.ppermute(tie(child_blocks, first), "front", swap)

    steps = sz.chunks + rows - 2
    columns_step = 0
    tiles_step = min(rows, steps - 1)
    settled_step = tiles_step + 2
    algebra_step = tiles_step + 3
    passed = ([], [])
    held = [panel_rows[0][0], panel_rows[1][0]]
    mine = tiles = columns = lower_1 = half = upper = lower = out = None
    exact, waits = [], []

    def invert_first():
        nonlocal lower_1, half
        x, half, lower_1 = first_inverse(plan, *tiles, exact_0)
        exact.append(x)
        return lower_1

    def invert_second():
        nonlocal half, upper
        x, second, upper = second_inverse(plan, *tiles, exact_1, lower_1)
        half = (half, second)
        exact.append(x)
        return second

    def all_multipliers():
        nonlocal lower
        lower = [multipliers(sz, plan, *columns, *half, upper, n) for n in range(PARTS)]
        return lower[-1]

    def updates(chunk, count):
        nonlocal out
        at = [passed[p][chunk : chunk + count + rows - 1] for p in range(2)]
        out = update(
            sz, plan, chunk, count, front_matrix, child_blocks, partner, lower, lower_1, at, exact, out
        )
        return out

    todo = [(0, invert_first), (0, invert_second), (0, all_multipliers)]
    chunk = 0
    while chunk < sz.chunks:
        count = TILE_CHUNKS if chunk + TILE_CHUNKS <= sz.chunks - TILE_CHUNKS else 1
        todo.append((chunk + count + rows - 2, functools.partial(updates, chunk, count)))
        chunk += count

    after = ()
    for s in range(steps):
        for k in range(2):
            if s and s < sz.chunks:
                held[k] = inject(flags[k], panel_rows[k][s], tie(held[k], *after))
            elif s:
                held[k] = tie(held[k], *after)
            after = ()
            passed[k].append(held[k])
            held[k] = lax.ppermute(held[k], "row", ring)
        last = passed[1][-1]
        if s == columns_step:
            mine = first_columns(sz, plan, front_matrix, child_blocks, tie(got_cols, last))
            columns = from_first_two(cols, col, mine)
            after = (mine,)
        if early < sz.chunks and s in (early - 2, early - 1):
            k = s - early + 2
            (more,), _ = pivot_chunks(
                sz, plan, front_matrix, child_blocks, tie(partner, last), (k,), early, sz.chunks - early
            )
            panel_rows[k] = panel_rows[k] + more
            after = (more[0],)
        if s == tiles_step:
            mine = gather_tiles(sz, plan, [passed[p][: TILE_CHUNKS + rows - 1] for p in range(2)])
            tiles = from_first_two(cols, col, mine)
            after = after + (mine,)
        if s == settled_step:
            columns = tie(columns, last)
            after = (columns[1],)
        if s == algebra_step:
            tiles = tie(tiles, last)
        if s >= algebra_step and todo[0][0] <= s:
            after = (todo.pop(0)[1](),)
    for k in range(2):
        passed[k].append(held[k])
    for _, piece in todo:
        piece()
    return out


def solution(mesh):
    in_specs = (P("front", "row", "col"), P("front", None, "row", "col"), P(), P())
    out_specs = P("front", "row", "col")
    step = functools.partial(body, mesh.shape["row"], mesh.shape["col"])
    return jax.shard_map(step, mesh=mesh, in_specs=in_specs, out_specs=out_specs, check_vma=False)
```

```python
import functools

import jax
import jax.numpy as jnp
from jax import lax
from jax.experimental import pallas as pl
from jax.experimental.pallas import tpu as pltpu
from jax.sharding import PartitionSpec as P

W = 512
MB = 128
CH = 256
PB = W // MB
TILE_CHUNKS = W // CH
EARLY_CHUNKS = 6
PARTS = 2
HBM = pl.BlockSpec(memory_space=pltpu.HBM)
SMEM = pl.BlockSpec(memory_space=pltpu.SMEM)
TILE_SPEC = pl.BlockSpec((W, W), lambda i: (0, 0))
TILES_SPEC = pl.BlockSpec((2, TILE_CHUNKS, W, CH), lambda i: (0, 0, 0, 0))
F32 = jnp.float32
BF16 = jnp.bfloat16
MIB = 1 << 20
VMEM_MIB = 48
FULL_MIB = 60
VMEM = pl.BlockSpec(memory_space=pltpu.VMEM)

OWNS, DIST, LOCAL, OWN_AT, GOT_AT, SEND_AT, COL, FLIP, LISTS = 0, 2, 4, 6, 8, 10, 12, 13, 16


class Sizes:
    def __init__(self, rows, cols, front, child):
        self.rows, self.cols = rows, cols
        self.local_rows, self.local_cols = front
        self.child_rows, self.child_cols = child
        self.row_blocks = self.local_rows // W
        self.chunks = self.local_cols // CH
        self.map_rows, self.map_cols = self.local_rows // MB, self.local_cols // MB
        self.own_row = LISTS
        self.got_row = self.own_row + self.map_rows
        self.own_col = self.got_row + self.map_rows
        self.got_col = self.own_col + self.map_cols
        self.plan = self.got_col + self.map_cols


def params(mib):
    return pltpu.CompilerParams(vmem_limit_bytes=mib * MIB)


def make_plan(sz, ids, child_maps, pivot_rows):
    child_row_blocks = sz.child_rows // MB
    child_col_blocks = sz.child_cols // MB

    def place(z):
        return jnp.where(z % 2 == 1, (z + 1) // 2, jnp.where(z == 0, 0, sz.rows - z // 2))

    def kernel(ids_ref, maps_ref, order_ref, out_ref):
        front, row, col = ids_ref[0], ids_ref[1], ids_ref[2]
        partner = jnp.bitwise_xor(front, 1)
        for i in range(FLIP + 1, LISTS):
            out_ref[i] = 0
        out_ref[COL] = col
        out_ref[FLIP] = col if sz.cols == 2 else jnp.int32(0)

        def start(f, s, local):
            count = jnp.int32(0)
            for b in range(child_row_blocks):
                at = maps_ref[f, s, row * child_row_blocks + b] - row * sz.map_rows
                count += (at < local * PB).astype(jnp.int32)
            return jnp.minimum(count, child_row_blocks - PB)

        for p in range(2):
            pivot = order_ref[front, p]
            owner = pivot // sz.row_blocks
            local = pivot - owner * sz.row_blocks
            other = order_ref[partner, p] % sz.row_blocks
            out_ref[OWNS + p] = (owner == row).astype(jnp.int32)
            out_ref[DIST + p] = (place(row) - place(owner) + sz.rows) % sz.rows
            out_ref[LOCAL + p] = local
            out_ref[OWN_AT + p] = start(front, 0, local)
            out_ref[GOT_AT + p] = start(partner, 1, local)
            out_ref[SEND_AT + p] = start(front, 1, other)
        for f, s, row_list, col_list in (
            (front, 0, sz.own_row, sz.own_col),
            (partner, 1, sz.got_row, sz.got_col),
        ):
            for i in range(sz.map_rows):
                out_ref[row_list + i] = -1
            for i in range(sz.map_cols):
                out_ref[col_list + i] = -1
            for b in range(child_row_blocks):
                at = maps_ref[f, s, row * child_row_blocks + b] - row * sz.map_rows
                out_ref[row_list + at] = b
            for b in range(child_col_blocks):
                at = maps_ref[f, s, col * child_col_blocks + b] - col * sz.map_cols
                out_ref[col_list + at] = b

    return pl.pallas_call(
        kernel,
        out_shape=jax.ShapeDtypeStruct((sz.plan,), jnp.int32),
        in_specs=[SMEM] * 3,
        out_specs=SMEM,
        compiler_params=params(FULL_MIB),
        name="plan",
    )(ids, child_maps, pivot_rows)


def cut_rows(sz, plan, child_blocks, columns):
    def kernel(plan_ref, child_ref, out_ref, sems):
        copies = []
        for p in range(2):
            at = pl.multiple_of(plan_ref[SEND_AT + p] * MB, MB)
            source = child_ref.at[0, 1, pl.ds(at, W), pl.ds(0, columns)]
            copies.append(pltpu.make_async_copy(source, out_ref.at[p], sems.at[p]))
            copies[-1].start()
        for copy in copies:
            copy.wait()

    return pl.pallas_call(
        kernel,
        out_shape=jax.ShapeDtypeStruct((2, W, columns), BF16),
        in_specs=[SMEM, HBM],
        out_specs=VMEM,
        scratch_shapes=[pltpu.SemaphoreType.DMA((2,))],
        compiler_params=params(VMEM_MIB),
        cost_estimate=pl.CostEstimate(flops=0, bytes_accessed=10 * MIB, transcendentals=0),
        name="cut_rows",
    )(plan, child_blocks)


def cut_cols(sz, child_blocks):
    def kernel(child_ref, out_ref, sem):
        copy = pltpu.make_async_copy(child_ref.at[0, 1, :, pl.ds(0, W)], out_ref, sem)
        copy.start()
        copy.wait()

    return pl.pallas_call(
        kernel,
        out_shape=jax.ShapeDtypeStruct((sz.child_rows, W), BF16),
        in_specs=[HBM],
        out_specs=VMEM,
        scratch_shapes=[pltpu.SemaphoreType.DMA],
        compiler_params=params(FULL_MIB),
        name="cut_cols",
    )(child_blocks)


def place_of(row, col):
    there = jnp.logical_and(row >= 0, col >= 0).astype(F32)
    row_at = pl.multiple_of(jnp.maximum(row, 0) * MB, MB)
    col_at = pl.multiple_of(jnp.maximum(col, 0) * MB, MB)
    return pl.ds(row_at, MB), pl.ds(col_at, MB), there


def pivot_chunks(sz, plan, front_matrix, child_blocks, got_rows, panels, first, count):
    whole = got_rows.ndim == 4
    columns = got_rows.shape[-1]
    tiles = TILE_CHUNKS if first == 0 else 0
    total = len(panels) * count
    exacts = len(panels) if tiles else 0

    def kernel(plan_ref, front_ref, child_ref, got_ref, *refs):
        rows_refs, exact_refs = refs[:total], refs[total : total + exacts]
        own_buf, got_buf, f_buf, o_buf, sems = refs[total + exacts :]
        children, loads, stores = [], [], []
        for n, p in enumerate(panels):
            at = pl.multiple_of(plan_ref[OWN_AT + p] * MB, MB)
            source = child_ref.at[0, 0, pl.ds(at, W), pl.ds(0, columns)]
            children.append(pltpu.make_async_copy(source, own_buf.at[n], sems.at[2 * n]))
            at = pl.multiple_of(plan_ref[GOT_AT + p] * MB, MB)
            source = got_ref.at[0, 1, pl.ds(at, W)] if whole else got_ref.at[p]
            children.append(pltpu.make_async_copy(source, got_buf.at[n], sems.at[2 * n + 1]))
        for copy in children:
            copy.start()
        for n, p in enumerate(panels):
            rows = pl.ds(pl.multiple_of(plan_ref[LOCAL + p] * W, W), W)
            for j in range(count):
                at = n * count + j
                base = 4 + 3 * at
                source = front_ref.at[0, rows, pl.ds((first + j) * CH, CH)]
                loads.append(pltpu.make_async_copy(source, f_buf.at[at], sems.at[base]))
                loads[-1].start()
                stores.append(
                    [pltpu.make_async_copy(o_buf.at[at], rows_refs[at], sems.at[base + 1])]
                )
                if j < tiles:
                    target = exact_refs[n].at[:, pl.ds(j * CH, CH)]
                    stores[-1].append(
                        pltpu.make_async_copy(f_buf.at[at], target, sems.at[base + 2])
                    )
        for copy in children:
            copy.wait()
        for n, p in enumerate(panels):
            own_at, got_at = plan_ref[OWN_AT + p], plan_ref[GOT_AT + p]
            local = plan_ref[LOCAL + p]
            for j in range(count):
                at = n * count + j
                loads[at].wait()
                for q in range(CH // MB):
                    here = pl.ds(q * MB, MB)
                    own_col = plan_ref[sz.own_col + (first + j) * (CH // MB) + q]
                    got_col = plan_ref[sz.got_col + (first + j) * (CH // MB) + q]
                    for i in range(PB):
                        own_row = plan_ref[sz.own_row + local * PB + i] - own_at
                        got_row = plan_ref[sz.got_row + local * PB + i] - got_at
                        r1, c1, f1 = place_of(own_row, own_col)
                        r2, c2, f2 = place_of(got_row, got_col)
                        value = f_buf[at, pl.ds(i * MB, MB), here]
                        value += own_buf[n, r1, c1].astype(F32) * f1
                        value += got_buf[n, r2, c2].astype(F32) * f2
                        o_buf[at, pl.ds(i * MB, MB), here] = value.astype(BF16)
                        if j < tiles:
                            f_buf[at, pl.ds(i * MB, MB), here] = value
                for copy in stores[at]:
                    copy.start()
        for group in stores:
            for copy in group:
                copy.wait()

    outs = pl.pallas_call(
        kernel,
        out_shape=[jax.ShapeDtypeStruct((W, CH), BF16)] * total
        + [jax.ShapeDtypeStruct((W, W), F32)] * exacts,
        in_specs=[SMEM, HBM, HBM, HBM],
        out_specs=[HBM] * (total + exacts),
        scratch_shapes=[
            pltpu.VMEM((len(panels), W, columns), BF16),
            pltpu.VMEM((len(panels), W, columns), BF16),
            pltpu.VMEM((total, W, CH), F32),
            pltpu.VMEM((total, W, CH), BF16),
            pltpu.SemaphoreType.DMA((4 + 3 * total,)),
        ],
        compiler_params=params(FULL_MIB),
        cost_estimate=pl.CostEstimate(flops=0, bytes_accessed=12 * MIB, transcendentals=0),
        name="pivot_chunks",
    )(plan, front_matrix, child_blocks, got_rows)
    return [outs[n * count : (n + 1) * count] for n in range(len(panels))], outs[total:]


def first_columns(sz, plan, front_matrix, child_blocks, got_cols):
    def kernel(plan_ref, front_ref, own_ref, got_ref, out_ref):
        r = pl.program_id(0)
        for i in range(PB):
            own_row = plan_ref[sz.own_row + r * PB + i]
            got_row = plan_ref[sz.got_row + r * PB + i]
            for q in range(PB):
                r1, c1, f1 = place_of(own_row, plan_ref[sz.own_col + q])
                r2, c2, f2 = place_of(got_row, plan_ref[sz.got_col + q])
                here = (pl.ds(i * MB, MB), pl.ds(q * MB, MB))
                value = front_ref[0, here[0], here[1]] + own_ref[r1, c1].astype(F32) * f1
                value += got_ref[r2, c2].astype(F32) * f2
                out_ref[here] = value.astype(BF16)

    return pl.pallas_call(
        kernel,
        out_shape=jax.ShapeDtypeStruct((sz.local_rows, W), BF16),
        grid_spec=pltpu.PrefetchScalarGridSpec(
            num_scalar_prefetch=1,
            grid=(sz.row_blocks,),
            in_specs=[
                pl.BlockSpec((1, W, W), lambda r, plan: (0, r, 0)),
                pl.BlockSpec((None, None, sz.child_rows, W), lambda r, plan: (0, 0, 0, 0)),
                pl.BlockSpec((sz.child_rows, W), lambda r, plan: (0, 0)),
            ],
            out_specs=pl.BlockSpec((W, W), lambda r, plan: (r, 0)),
        ),
        compiler_params=params(FULL_MIB),
        cost_estimate=pl.CostEstimate(flops=0, bytes_accessed=12 * MIB, transcendentals=0),
        name="first_columns",
    )(plan, front_matrix, child_blocks, got_cols)


def inject(flag, rows, received):
    def kernel(flag_ref, rows_ref, received_ref, out_ref, held_ref, sems):
        @pl.when(flag_ref[0] == 1)
        def _():
            for n, (source, target) in enumerate(((rows_ref, held_ref), (held_ref, out_ref))):
                copy = pltpu.make_async_copy(source, target, sems.at[n])
                copy.start()
                copy.wait()

    return pl.pallas_call(
        kernel,
        out_shape=jax.ShapeDtypeStruct(received.shape, BF16),
        in_specs=[SMEM, HBM, HBM],
        out_specs=HBM,
        scratch_shapes=[pltpu.VMEM(received.shape, BF16), pltpu.SemaphoreType.DMA((2,))],
        input_output_aliases={2: 0},
        compiler_params=params(VMEM_MIB),
        name="inject",
    )(flag, rows, received)


def gather_tiles(sz, plan, passed):
    count = len(passed[0])

    def kernel(plan_ref, *refs):
        sources = (refs[:count], refs[count : 2 * count])
        out_ref, sems = refs[2 * count :]
        for p in range(2):
            for d in range(sz.rows):

                @pl.when(plan_ref[DIST + p] == d)
                def _():
                    for t in range(TILE_CHUNKS):
                        pltpu.make_async_copy(
                            sources[p][t + d], out_ref.at[p, t], sems.at[p, t]
                        ).start()

        for p in range(2):
            for t in range(TILE_CHUNKS):
                pltpu.make_async_copy(sources[p][t], out_ref.at[p, t], sems.at[p, t]).wait()

    return pl.pallas_call(
        kernel,
        out_shape=jax.ShapeDtypeStruct((2, TILE_CHUNKS, W, CH), BF16),
        in_specs=[SMEM] + [HBM] * (2 * count),
        out_specs=VMEM,
        scratch_shapes=[pltpu.SemaphoreType.DMA((2, TILE_CHUNKS))],
        compiler_params=params(FULL_MIB),
        name="gather_tiles",
    )(plan, *passed[0], *passed[1])


def split(value):
    high = value.astype(BF16)
    return high, (value - high.astype(F32)).astype(BF16)


def product_of(a, b):
    dot = functools.partial(jnp.dot, preferred_element_type=F32)
    return dot(a[0], b[0]) + (dot(a[0], b[1]) + dot(a[1], b[0]))


def invert(block):
    rows = lax.broadcasted_iota(jnp.int32, (W, W), 0)
    cols = lax.broadcasted_iota(jnp.int32, (W, W), 1)
    on_diagonal = rows == cols
    diagonal = jnp.where(on_diagonal, block, 0.0)
    down = 1.0 / jnp.sum(diagonal, axis=1, keepdims=True)
    across = 1.0 / jnp.sum(diagonal, axis=0, keepdims=True)
    first = jnp.where(on_diagonal, 2.0 * down, 0.0) - down * block * across
    halves = split(first)
    return 2.0 * first - product_of(halves, split(product_of(split(block), halves)))


def tiles_of(plan_ref, mine_ref, other_ref, col, p):
    flip = plan_ref[FLIP] == 1 - col
    pair = [jnp.where(flip, other_ref[p, t], mine_ref[p, t]) for t in range(TILE_CHUNKS)]
    return jnp.concatenate(pair, axis=1)


def first_inverse(plan, mine, other, exact):
    def kernel(plan_ref, mine_ref, other_ref, exact_ref, x_ref, h_ref, l_ref):
        here = jnp.logical_and(plan_ref[OWNS] == 1, plan_ref[COL] == 0)
        tile = tiles_of(plan_ref, mine_ref, other_ref, 0, 0).astype(F32)
        x = invert(jnp.where(here, exact_ref[...], tile))
        x_ref[...] = x
        h_ref[...] = x.astype(BF16)
        tile = tiles_of(plan_ref, mine_ref, other_ref, 0, 1)
        l_ref[...] = jnp.dot(tile, h_ref[...], preferred_element_type=F32).astype(BF16)

    return pl.pallas_call(
        kernel,
        out_shape=[jax.ShapeDtypeStruct((W, W), t) for t in (F32, BF16, BF16)],
        grid=(1,),
        in_specs=[SMEM] + [TILES_SPEC] * 2 + [TILE_SPEC] * 1,
        out_specs=[TILE_SPEC] * 3,
        compiler_params=params(VMEM_MIB),
        cost_estimate=pl.CostEstimate(flops=1 << 32, bytes_accessed=4 * MIB, transcendentals=0),
        name="first_inverse",
    )(plan, mine, other, exact)


def second_inverse(plan, mine, other, exact, lower_1):
    def kernel(plan_ref, mine_ref, other_ref, exact_ref, l_ref, x_ref, h_ref, u_ref):
        here = jnp.logical_and(plan_ref[OWNS + 1] == 1, plan_ref[COL] == 1)
        u_ref[...] = tiles_of(plan_ref, mine_ref, other_ref, 1, 0)
        tile = tiles_of(plan_ref, mine_ref, other_ref, 1, 1).astype(F32)
        block = jnp.where(here, exact_ref[...], tile)
        x = invert(block - jnp.dot(l_ref[...], u_ref[...], preferred_element_type=F32))
        x_ref[...] = x
        h_ref[...] = x.astype(BF16)

    return pl.pallas_call(
        kernel,
        out_shape=[jax.ShapeDtypeStruct((W, W), t) for t in (F32, BF16, BF16)],
        grid=(1,),
        in_specs=[SMEM] + [TILES_SPEC] * 2 + [TILE_SPEC] * 2,
        out_specs=[TILE_SPEC] * 3,
        compiler_params=params(VMEM_MIB),
        cost_estimate=pl.CostEstimate(flops=1 << 32, bytes_accessed=4 * MIB, transcendentals=0),
        name="second_inverse",
    )(plan, mine, other, exact, lower_1)


def is_pivot(plan_ref, panel, r):
    return jnp.logical_and(plan_ref[OWNS + panel] == 1, plan_ref[LOCAL + panel] == r)


def multipliers(sz, plan, mine, other, half_0, half_1, upper, part):
    steps = sz.row_blocks // PARTS

    def kernel(plan_ref, mine_ref, other_ref, h0_ref, h1_ref, u_ref, out_ref):
        r = pl.program_id(0) + part * steps
        flip = plan_ref[FLIP] == 1
        keep_0 = 1.0 - is_pivot(plan_ref, 0, r).astype(F32)
        keep_1 = keep_0 * (1.0 - is_pivot(plan_ref, 1, r).astype(F32))
        first = jnp.where(flip, other_ref[...], mine_ref[...])
        lower_0 = jnp.dot(first, h0_ref[...], preferred_element_type=F32) * keep_0
        lower_0 = lower_0.astype(BF16)
        column = jnp.where(flip, mine_ref[...], other_ref[...]).astype(F32)
        column -= jnp.dot(lower_0, u_ref[...], preferred_element_type=F32)
        lower_1 = jnp.dot(column.astype(BF16), h1_ref[...], preferred_element_type=F32) * keep_1
        out_ref[:, :W] = lower_0
        out_ref[:, W:] = lower_1.astype(BF16)

    rows = pl.BlockSpec((W, W), lambda r, plan: (r + part * steps, 0))
    return pl.pallas_call(
        kernel,
        out_shape=jax.ShapeDtypeStruct((steps * W, 2 * W), BF16),
        grid_spec=pltpu.PrefetchScalarGridSpec(
            num_scalar_prefetch=1,
            grid=(steps,),
            in_specs=[rows, rows, VMEM, VMEM, VMEM],
            out_specs=pl.BlockSpec((W, 2 * W), lambda r, plan: (r, 0)),
        ),
        compiler_params=params(VMEM_MIB),
        cost_estimate=pl.CostEstimate(
            flops=6 * steps * W * W * W, bytes_accessed=5 * MIB, transcendentals=0
        ),
        name="multipliers",
    )(plan, mine, other, half_0, half_1, upper)


def tie(value, *after):
    return lax.optimization_barrier((value, *after))[0]


def update(
    sz, plan, chunk, count, front_matrix, child_blocks, partner, lower, lower_1, passed, exact, out
):
    special = chunk == 0
    width = count * CH
    per = width // MB
    start = chunk * CH // MB
    blocks = sz.row_blocks
    columns = pl.ds(chunk * CH, width)
    span = count + sz.rows - 1

    def kernel(plan_ref, front_ref, own_ref, partner_ref, *refs):
        l_refs, low_ref, refs = refs[:PARTS], refs[PARTS], refs[PARTS + 1 :]
        sources = (refs[:span], refs[span : 2 * span])
        refs = refs[2 * span :]
        if special:
            exact_refs, refs = refs[:2], refs[2:]
        out_ref, f_buf, c_buf, x_buf, upper, raw, o_buf, sems = refs[-8:]
        targets = (upper.at[pl.ds(0, W)], raw)

        def fetch(p, c, d):
            return pltpu.make_async_copy(
                sources[p][c + d], targets[p].at[:, pl.ds(c * CH, CH)], sems.at[p * count + c]
            )

        for p in range(2):
            for d in range(sz.rows):

                @pl.when(plan_ref[DIST + p] == d)
                def _():
                    for c in range(count):
                        fetch(p, c, d).start()

        head = [fetch(p, c, 0) for p in range(2) for c in range(count)]
        children = []
        for n, (child, which, at) in enumerate(
            ((own_ref, 0, sz.own_col), (partner_ref, 1, sz.got_col))
        ):
            for q in range(per):
                b = jnp.maximum(plan_ref[at + start + q], 0)
                b = pl.ds(pl.multiple_of(b * MB, MB), MB)
                children.append(
                    pltpu.make_async_copy(
                        child.at[0, which, :, b], c_buf.at[n, q], sems.at[2 * count + n * per + q]
                    )
                )
                children[-1].start()
        base = 2 * count + 2 * per
        if special:
            for p in range(2):
                children.append(
                    pltpu.make_async_copy(
                        exact_refs[p].at[:, columns], x_buf.at[p], sems.at[base + p]
                    )
                )
                children[-1].start()
        base += 2
        loads, stores = [], []
        for r in range(blocks):
            rows = pl.ds(r * W, W)
            loads.append(
                pltpu.make_async_copy(
                    front_ref.at[0, rows, columns], f_buf.at[rows], sems.at[base + 2 * r]
                )
            )
            stores.append(
                pltpu.make_async_copy(
                    o_buf.at[rows], out_ref.at[0, rows, columns], sems.at[base + 2 * r + 1]
                )
            )
            loads[-1].start()
        for copy in head:
            copy.wait()
        product = jnp.dot(low_ref[...], upper[:W], preferred_element_type=F32)
        upper[W:] = (raw[...].astype(F32) - product).astype(BF16)
        for r in range(blocks):
            l_ref, l_rows = l_refs[r // (blocks // PARTS)], pl.ds(r % (blocks // PARTS) * W, W)
            product = jnp.dot(l_ref[l_rows], upper[...], preferred_element_type=F32)
            for copy in children if r == 0 else ():
                copy.wait()
            loads[r].wait()
            for q in range(per):
                here = pl.ds(q * MB, MB)
                own_col = plan_ref[sz.own_col + start + q]
                got_col = plan_ref[sz.got_col + start + q]
                for i in range(PB):
                    rows = pl.ds(r * W + i * MB, MB)
                    r1, _, f1 = place_of(plan_ref[sz.own_row + r * PB + i], own_col)
                    r2, _, f2 = place_of(plan_ref[sz.got_row + r * PB + i], got_col)
                    value = f_buf[rows, here] + c_buf[0, q, r1, :].astype(F32) * f1
                    value += c_buf[1, q, r2, :].astype(F32) * f2
                    value -= product[i * MB : (i + 1) * MB, q * MB : (q + 1) * MB]
                    o_buf[rows, here] = value
            if special:
                col = plan_ref[COL]
                first, second = is_pivot(plan_ref, 0, r), is_pivot(plan_ref, 1, r)
                rows = pl.ds(r * W, W)

                @pl.when(jnp.logical_and(col == 0, first))
                def _():
                    o_buf[rows] = x_buf[0]

                @pl.when(jnp.logical_and(col == 0, jnp.logical_not(first)))
                def _():
                    o_buf[rows] = l_ref[l_rows, columns].astype(F32)

                @pl.when(jnp.logical_and(col == 1, second))
                def _():
                    o_buf[rows] = x_buf[1]

                @pl.when(jnp.logical_and(col == 1, jnp.logical_not(jnp.logical_or(first, second))))
                def _():
                    o_buf[rows] = l_ref[l_rows, pl.ds(W, width)].astype(F32)

            stores[r].start()
        for copy in stores:
            copy.wait()

    operands = [plan, front_matrix, child_blocks, partner, *lower, lower_1]
    operands += list(passed[0]) + list(passed[1])
    if special:
        operands += list(exact)
    aliases = {}
    if out is not None:
        aliases = {len(operands): 0}
        operands.append(out)
    return pl.pallas_call(
        kernel,
        out_shape=jax.ShapeDtypeStruct(front_matrix.shape, F32),
        in_specs=[SMEM] + [HBM] * 3 + [VMEM] * (PARTS + 1) + [HBM] * (len(operands) - PARTS - 5),
        out_specs=HBM,
        scratch_shapes=[
            pltpu.VMEM((sz.local_rows, width), F32),
            pltpu.VMEM((2, per, sz.child_rows, MB), BF16),
            pltpu.VMEM((2, W, width), F32),
            pltpu.VMEM((2 * W, width), BF16),
            pltpu.VMEM((W, width), BF16),
            pltpu.VMEM((sz.local_rows, width), F32),
            pltpu.SemaphoreType.DMA((2 * count + 2 * per + 2 + 2 * blocks,)),
        ],
        input_output_aliases=aliases,
        compiler_params=params(VMEM_MIB),
        cost_estimate=pl.CostEstimate(
            flops=4 * sz.local_rows * W * width, bytes_accessed=8 * count * MIB, transcendentals=0
        ),
        name="update",
    )(*operands)


def tie(value, *after):
    return lax.optimization_barrier((value, *after))[0]


def from_first_two(cols, col, mine):
    if cols == 2:
        return mine, lax.ppermute(mine, "col", [(0, 1), (1, 0)])
    zero = jnp.zeros_like(mine)
    return tuple(lax.psum(jnp.where(col == c, mine, zero), "col") for c in range(2))


def body(rows, cols, front_matrix, child_blocks, child_maps, pivot_rows):
    sz = Sizes(rows, cols, front_matrix.shape[1:], child_blocks.shape[2:])
    front_count = lax.axis_size("front")
    swap = [(f, f ^ 1) for f in range(front_count)]
    order = [0] + list(range(1, rows, 2)) + sorted(range(2, rows, 2), reverse=True)
    ring = [(order[i], order[(i + 1) % rows]) for i in range(rows)]
    front, row, col = (lax.axis_index(a).astype(jnp.int32) for a in ("front", "row", "col"))
    ids = jnp.stack([front, row, col])
    plan = make_plan(sz, ids, child_maps, pivot_rows)
    pivots = lax.dynamic_index_in_dim(pivot_rows, front, 0, keepdims=False)
    flags = [(pivots[k : k + 1] // sz.row_blocks == row).astype(jnp.int32) for k in range(2)]

    early = min(EARLY_CHUNKS, sz.chunks)
    sent = cut_rows(sz, plan, child_blocks, min(early * CH, sz.child_cols))
    got = lax.ppermute(sent, "front", swap)
    got_cols = lax.ppermute(cut_cols(sz, tie(child_blocks, sent)), "front", swap)
    panel_rows, (exact_0, exact_1) = pivot_chunks(
        sz, plan, front_matrix, child_blocks, tie(got, got_cols), (0, 1), 0, early
    )
    first = panel_rows[0][0]
    partner = lax.ppermute(tie(child_blocks, first), "front", swap)

    steps = sz.chunks + rows - 2
    columns_step = 0
    tiles_step = min(rows, steps - 1)
    settled_step = tiles_step + 2
    algebra_step = tiles_step + 3
    passed = ([], [])
    held = [panel_rows[0][0], panel_rows[1][0]]
    mine = tiles = columns = lower_1 = half = upper = lower = out = None
    exact, waits = [], []

    def invert_first():
        nonlocal lower_1, half
        x, half, lower_1 = first_inverse(plan, *tiles, exact_0)
        exact.append(x)
        return lower_1

    def invert_second():
        nonlocal half, upper
        x, second, upper = second_inverse(plan, *tiles, exact_1, lower_1)
        half = (half, second)
        exact.append(x)
        return second

    def all_multipliers():
        nonlocal lower
        lower = [multipliers(sz, plan, *columns, *half, upper, n) for n in range(PARTS)]
        return lower[-1]

    def updates(chunk, count):
        nonlocal out
        at = [passed[p][chunk : chunk + count + rows - 1] for p in range(2)]
        out = update(
            sz, plan, chunk, count, front_matrix, child_blocks, partner, lower, lower_1, at, exact, out
        )
        return out

    todo = [(0, invert_first), (0, invert_second), (0, all_multipliers)]
    chunk = 0
    while chunk < sz.chunks:
        count = TILE_CHUNKS if chunk + TILE_CHUNKS <= sz.chunks - TILE_CHUNKS else 1
        todo.append((chunk + count + rows - 2, functools.partial(updates, chunk, count)))
        chunk += count

    after = ()
    for s in range(steps):
        for k in range(2):
            if s and s < sz.chunks:
                held[k] = inject(flags[k], panel_rows[k][s], tie(held[k], *after))
            elif s:
                held[k] = tie(held[k], *after)
            after = ()
            passed[k].append(held[k])
            held[k] = lax.ppermute(held[k], "row", ring)
        last = passed[1][-1]
        if s == columns_step:
            mine = first_columns(sz, plan, front_matrix, child_blocks, tie(got_cols, last))
            columns = from_first_two(cols, col, mine)
            after = (mine,)
        if early < sz.chunks and s in (early - 3, early - 2):
            k = s - early + 3
            (more,), _ = pivot_chunks(
                sz, plan, front_matrix, child_blocks, tie(partner, last), (k,), early, sz.chunks - early
            )
            panel_rows[k] = panel_rows[k] + more
            after = (more[0],)
        if s == tiles_step:
            mine = gather_tiles(sz, plan, [passed[p][: TILE_CHUNKS + rows - 1] for p in range(2)])
            tiles = from_first_two(cols, col, mine)
            after = after + (mine,)
        if s == settled_step:
            columns = tie(columns, last)
            after = (columns[1],)
        if s == algebra_step:
            tiles = tie(tiles, last)
        if s >= algebra_step and todo[0][0] <= s:
            after = (todo.pop(0)[1](),)
    for k in range(2):
        passed[k].append(held[k])
    for _, piece in todo:
        piece()
    return out


def solution(mesh):
    in_specs = (P("front", "row", "col"), P("front", None, "row", "col"), P(), P())
    out_specs = P("front", "row", "col")
    step = functools.partial(body, mesh.shape["row"], mesh.shape["col"])
    return jax.shard_map(step, mesh=mesh, in_specs=in_specs, out_specs=out_specs, check_vma=False)
```
